128 devices in a mesh: wave: 16 (over y, z), lev: 8 (over x, core).
Axes of the slice: x: 4, y: 4, z: 4, core: 2. Of those that a mesh axis runs over, the one named last changes fastest.
Arguments:
- spectral: bfloat16 [1280, 512, 1280], P('wave', 'lev'), may hold values from -6 to 6
- legendre: bfloat16 [1280, 128, 1280], P('wave'), may hold values from -0.0034179688 to 0.0034179688
- wave_map: int32 [1280], replicated, may hold values from 0 to 1279, each once
- row_points: int32 [128], replicated, may hold values from 20 to 5136, as said below
- brackets: int32 [8], replicated, may hold values from 0 to 30, as said below
- lev_weight: float32 [8], replicated, may hold values from 0.05 to 0.95
- climatology: float32 [8, 256, 5248], P('lev', 'wave'), may hold values from 0.1 to 1
Outputs:
- anomaly: float32 [8, 256, 5248], P('lev', 'wave')
The draws below stay inside these ranges and needn't reach their ends.
Inputs may be any that keep to these rules, and one draw needn't show every extreme that they name: `wave_map`: each wavenumber once. `row_points`: each is 20 + 4 i for a whole number i below 1280; some row has 5136 points. `brackets`: pressure level p has its lower bracket level among the 4 model levels of band p (levels b * 4 to b * 4 + 3 for band b); some pressure level outside the last band takes the last level of its band; the last pressure level takes 32 - 2.
All inputs are finite; a program needn't handle non-finite values.
Results may differ from the reference program's by a relative error of at most 0.0003.
Values sent between devices are 32-bit elements; how exact they have to be, the bound alone decides.
A program may use at most 256 MiB of HBM per device.

```python
import math
import jax
import jax.numpy as jnp
from jax import lax

M = 1280
NT = 1280
LEV_DEV = 4
PLEV_DEV = 1
STEPS = 4
FIELDS = 2
LEVELS = 32
PLEV = 8
COLS = 512
HALF = 128
LAT = 256
ROWPAD = 5248


def draw_row_points(key, part):
    key = jax.random.fold_in(key, 11)
    seed_draw, seed_place = jax.random.split(key)
    uniform_ids = jax.random.randint(seed_draw, (HALF,), 0, M)
    row_index = uniform_ids * uniform_ids // M
    chosen = jax.random.randint(seed_place, (), 0, HALF)
    row_index = jnp.where(jnp.arange(HALF) == chosen, M - 1, row_index)
    return (20 + 4 * row_index).astype(jnp.int32)


def draw_brackets(key, part):
    key = jax.random.fold_in(key, 57)
    seed_draw, seed_place = jax.random.split(key, 2)
    plev_ids = jnp.arange(PLEV, dtype=jnp.int32)
    band_ids = plev_ids // PLEV_DEV
    offsets = jax.random.randint(seed_draw, (PLEV,), 0, LEV_DEV)
    lower_ids = band_ids * LEV_DEV + offsets
    chosen = jax.random.randint(seed_place, (), 0, PLEV - PLEV_DEV)
    lower_ids = jnp.where(plev_ids == chosen, band_ids * LEV_DEV + LEV_DEV - 1, lower_ids)
    lower_ids = jnp.minimum(lower_ids, LEVELS - 2)
    lower_ids = jnp.where(plev_ids == PLEV - 1, LEVELS - 2, lower_ids)
    return lower_ids.astype(jnp.int32)


def levels(own_key, extent, pieces, least, top_value):
    gain = 1.0
    for axis_at, shards_of in pieces:
        heights = jax.random.uniform(jax.random.fold_in(jax.random.fold_in(own_key, 6), axis_at), (shards_of,), jnp.float32, least / len(pieces), top_value / len(pieces))
        gain = gain * jnp.repeat(jnp.exp(heights), extent[axis_at] // shards_of).reshape((-1,) + (1,) * (len(extent) - 1 - axis_at))
    return gain


def bell_draw(rng, shape, spread, limit, cuts=(), kind=jnp.bfloat16):
    array = spread * jax.random.normal(rng, shape, jnp.float32)
    if cuts:
        array = array * levels(rng, shape, cuts, -0.22, 0.18)
    return jnp.clip(array, -limit, limit).astype(kind)


def setup_inputs(seed: int = 0) -> dict:
    seeds = jax.random.split(jax.random.key(seed), 8)
    return {
        "spectral": bell_draw(seeds[0], (M, COLS, NT), 1.0, 6.0, ((0, 16), (1, 8))),
        "legendre": bell_draw(seeds[1], (M, HALF, NT), (2 * M * NT) ** -0.5, 0.0034179688, ((0, 16),)),
        "wave_map": jax.random.permutation(seeds[2], M).astype(jnp.int32),
        "row_points": draw_row_points(jax.random.fold_in(seeds[7], 71), 0),
        "brackets": draw_brackets(jax.random.fold_in(seeds[7], 71), 0),
        "lev_weight": jnp.clip(jax.random.uniform(seeds[5], (PLEV,), jnp.float32, 0.05, 0.95), 0.05, 0.95),
        "climatology": jnp.clip(0.1 + 0.9 * jax.random.uniform(seeds[6], (PLEV, LAT, ROWPAD), jnp.float32) ** levels(seeds[6], (PLEV, LAT, ROWPAD), ((0, 8), (1, 16)), -0.2, 0.2), 0.1, 1.0),
    }


TWO_PI = 2.0 * math.pi


def synthesize(coeffs, wave_map, points):
    wave_ids = wave_map.astype(jnp.int32)
    places = jnp.arange(ROWPAD, dtype=jnp.int32)
    phase_index = (wave_ids[:, None] * places[None, :]) % points
    angle_rad = phase_index.astype(jnp.float32) * (TWO_PI / points.astype(jnp.float32))
    live_mask = (wave_ids[:, None] <= (points - 1) // 2) & (places[None, :] < points)
    factor = jnp.where(wave_ids == 0, 1.0, 2.0).astype(jnp.float32)[:, None]
    cosine = jnp.where(live_mask, factor * jnp.cos(angle_rad), 0.0)
    sine_part = jnp.where(live_mask, -factor * jnp.sin(angle_rad), 0.0)
    basis_table = jnp.stack([cosine, sine_part], axis=1)
    return lax.dot_general(coeffs, basis_table, (((0, 2), (0, 1)), ((), ())),
                           precision=lax.Precision.HIGHEST, preferred_element_type=jnp.float32)


def kinetic(values):
    return 0.5 * jnp.mean(values[:, 0] * values[:, 0] + values[:, 1] * values[:, 1], axis=1)


def mixing_table(brackets, lev_weight, levels_all):
    level_ids = jnp.arange(levels_all, dtype=jnp.int32)
    lower_hit = (level_ids[None, :] == brackets[:, None]).astype(jnp.float32)
    upper_hit = (level_ids[None, :] == brackets[:, None] + 1).astype(jnp.float32)
    return lev_weight[:, None] * lower_hit + (1.0 - lev_weight[:, None]) * upper_hit


def reference(spectral, legendre, wave_map, row_points, brackets, lev_weight, climatology):
    mixing = mixing_table(brackets, lev_weight, LEVELS)
    degree = jnp.arange(NT, dtype=jnp.int32)
    width_q = FIELDS * STEPS * 2
    span_slots = 64

    def slot_block(first_slot):
        spec_part = lax.dynamic_slice_in_dim(spectral, first_slot, span_slots, 0)
        leg_part = lax.dynamic_slice_in_dim(legendre, first_slot, span_slots, 0).astype(jnp.float32)
        waves_part = lax.dynamic_slice_in_dim(wave_map, first_slot, span_slots, 0).astype(jnp.int32)
        kept_mask = degree[None, :] >= waves_part[:, None]
        parity = (1 - 2 * ((degree[None, :] + waves_part[:, None]) % 2)).astype(jnp.float32)
        plain_coeffs = jnp.where(kept_mask[:, None, :], spec_part.astype(jnp.float32), 0.0)
        signed = plain_coeffs * parity[:, None, :]
        north_part = jnp.einsum("scn,sjn->scj", plain_coeffs, leg_part, precision=lax.Precision.HIGHEST)
        south_part = jnp.einsum("scn,sjn->scj", signed, leg_part, precision=lax.Precision.HIGHEST)
        fourier = jnp.concatenate([north_part, south_part], axis=2).reshape(span_slots, LEVELS, width_q, LAT)
        return jnp.einsum("pl,slqr->rspq", mixing, fourier, precision=lax.Precision.HIGHEST)

    starts = jnp.arange(0, M, span_slots, dtype=jnp.int32)
    blocks_out = lax.map(slot_block, starts)
    coeffs = jnp.transpose(blocks_out, (1, 0, 2, 3, 4)).reshape(LAT, M, PLEV * FIELDS * STEPS, 2)
    points_all = jnp.concatenate([row_points, row_points]).astype(jnp.int32)

    def row_energy(row_input):
        row_coeffs, points = row_input
        grid_row = synthesize(row_coeffs, wave_map, points).reshape(PLEV, FIELDS, STEPS, ROWPAD)
        return kinetic(grid_row)

    energy = jnp.transpose(lax.map(row_energy, (coeffs, points_all)), (1, 0, 2))
    places = jnp.arange(ROWPAD, dtype=jnp.int32)
    inside = places[None, None, :] < points_all[None, :, None]
    return jnp.where(inside, energy - climatology, 0.0)
```

```python
import functools
import math

import jax
import jax.numpy as jnp
from jax import lax
from jax.experimental import pallas as pl
from jax.experimental.pallas import tpu as pltpu
from jax.sharding import PartitionSpec as P

MESH = pl.DeviceIdType.MESH

M = 1280
NT = 1280
LEV_DEV = 4
COLS = 16
HALF = 128
ROWPAD = 5248
LANES = 128

WAVES = 16
LEVS = 8
DEVICES = WAVES * LEVS
SLOTS = M // WAVES
STEP_SLOTS = 8
STEPS = SLOTS // STEP_SLOTS
GROUPS = SLOTS // 4
PACK = 24
PER_SLOT = 2 * COLS

KBLOCK = 128
KBLOCKS = 11
KSPAN = KBLOCK * KBLOCKS
TILES = ROWPAD // LANES
ROWTILES = 48

NT_DIMS = (((1,), (1,)), ((), ()))


def flat_id():
    return lax.axis_index("wave") * LEVS + lax.axis_index("lev")


def pair_of(wave, lev):
    return (wave % 8) * 16 + (wave // 8) * 8 + lev


def transform_kernel(
    waves_ref, brackets_ref, weight_ref, spec_ref, leg_ref, recv_ref,
    mixed, first, other, send, near_send, near_recv, far_send, far_recv, own_sem,
):
    step = pl.program_id(0)
    wave, lev = lax.axis_index("wave"), lax.axis_index("lev")
    me = wave * LEVS + lev
    below = lax.rem(lev + LEVS - 1, LEVS)
    barrier = pltpu.get_barrier_semaphore()

    @pl.when(step == 0)
    def _():
        def greet(d, carry):
            target = lax.rem(me + d, DEVICES)
            pl.semaphore_signal(
                barrier, inc=1, device_id=(target // LEVS, lax.rem(target, LEVS)), device_id_type=MESH
            )
            return carry

        lax.fori_loop(1, DEVICES, greet, 0)
        for g in range(GROUPS, PACK):
            send[pl.ds(g, HALF, stride=PACK), :] = jnp.zeros((HALF, LANES), jnp.float32)

    lower = brackets_ref[lev] - lev * LEV_DEV
    weight = weight_ref[lev]
    level_weight = []
    for level in range(LEV_DEV):
        share = jnp.where(lower == level, weight, 0.0) + jnp.where(lower + 1 == level, 1.0 - weight, 0.0)
        level_weight.append(share)
    gain = jnp.where(lower == LEV_DEV - 1, 1.0 - weight, 0.0)

    degree = lax.broadcasted_iota(jnp.int32, (1, NT), 1)
    for i in range(STEP_SLOTS):
        order = waves_ref[wave * SLOTS + step * STEP_SLOTS + i]
        kept = jnp.where(degree >= order, 1.0, 0.0)
        signed = kept * (1 - 2 * ((degree + order) & 1)).astype(jnp.float32)
        coeffs = spec_ref[i]
        both = jnp.concatenate(
            [coeffs * kept.astype(jnp.bfloat16), coeffs * signed.astype(jnp.bfloat16)], axis=0
        )
        sums = lax.dot_general(both, leg_ref[i], NT_DIMS, preferred_element_type=jnp.float32)
        base = (step * STEP_SLOTS + i) * PER_SLOT
        for hemi in range(2):
            own = [sums[(hemi * LEV_DEV + v) * COLS : (hemi * LEV_DEV + v + 1) * COLS] for v in range(LEV_DEV)]
            total = own[0] * level_weight[0]
            for v in range(1, LEV_DEV):
                total = total + own[v] * level_weight[v]
            at = pl.ds(pl.multiple_of(base + hemi * COLS, COLS), COLS)
            mixed[at, :] = total
            first[at, :] = own[0]

    def near_copy(t):
        rows = pl.ds(pl.multiple_of(t * (STEP_SLOTS * PER_SLOT), STEP_SLOTS * PER_SLOT), STEP_SLOTS * PER_SLOT)
        return pltpu.make_async_remote_copy(
            src_ref=first.at[rows],
            dst_ref=other.at[rows],
            send_sem=near_send.at[t],
            recv_sem=near_recv.at[t],
            device_id=(wave, below),
            device_id_type=MESH,
        )

    @pl.when(step == 0)
    def _():
        pl.semaphore_wait(barrier, DEVICES - 1)

    near_copy(step).start()

    def assemble(g, carry):
        pieces = []
        for c in range(8):
            b = lax.rem(c - lev + 8, 8)
            base = (4 * g + b // 2) * PER_SLOT + lax.rem(b, 2)
            for hemi in range(2):
                at = pl.ds(base + hemi * COLS, 8, stride=2)
                pieces.append(mixed[at, :] + gain * other[at, :])
        block = jnp.concatenate(pieces, axis=0)
        send[pl.ds(g, HALF, stride=PACK), :] = block.T
        return carry

    @pl.when(step == STEPS - 1)
    def _():
        for t in range(STEPS):
            near_copy(t).wait_recv()
            lax.fori_loop(2 * t, 2 * t + 2, assemble, 0)

        def far_copy(d):
            target = lax.rem(me + d, DEVICES)
            to_wave, to_lev = target // LEVS, lax.rem(target, LEVS)
            at = pl.multiple_of(pair_of(to_wave, to_lev) * PACK, 8)
            return pltpu.make_async_remote_copy(
                src_ref=send.at[pl.ds(at, PACK)],
                dst_ref=recv_ref.at[me],
                send_sem=far_send,
                recv_sem=far_recv,
                device_id=(to_wave, to_lev),
                device_id_type=MESH,
            )

        def push(d, carry):
            far_copy(d).start()
            return carry

        lax.fori_loop(1, DEVICES, push, 0)
        mine = pltpu.make_async_copy(
            send.at[pl.ds(pl.multiple_of(pair_of(wave, lev) * PACK, 8), PACK)], recv_ref.at[me], own_sem
        )
        mine.start()
        mine.wait()
        for t in range(STEPS):
            near_copy(t).wait_send()
        all_out = send.at[pl.ds(0, (DEVICES - 1) * PACK)]
        pltpu.make_async_copy(all_out, all_out, far_send).wait()
        all_in = recv_ref.at[pl.ds(0, DEVICES - 1)]
        pltpu.make_async_copy(all_in, all_in, far_recv).wait()


def transform(wave_map, brackets, lev_weight, spectral, legendre):
    smem = pl.BlockSpec(memory_space=pltpu.SMEM)
    rows = SLOTS * PER_SLOT
    return pl.pallas_call(
        transform_kernel,
        grid=(STEPS,),
        out_shape=jax.ShapeDtypeStruct((DEVICES, PACK, LANES), jnp.float32),
        in_specs=[
            smem,
            smem,
            smem,
            pl.BlockSpec((STEP_SLOTS, LEV_DEV * COLS, NT), lambda t: (t, 0, 0)),
            pl.BlockSpec((STEP_SLOTS, HALF, NT), lambda t: (t, 0, 0)),
        ],
        out_specs=pl.BlockSpec(memory_space=pl.ANY),
        scratch_shapes=[
            pltpu.VMEM((rows, HALF), jnp.float32),
            pltpu.VMEM((rows, HALF), jnp.float32),
            pltpu.VMEM((rows, HALF), jnp.float32),
            pltpu.VMEM((HALF * PACK, LANES), jnp.float32),
            pltpu.SemaphoreType.DMA((STEPS,)),
            pltpu.SemaphoreType.DMA((STEPS,)),
            pltpu.SemaphoreType.DMA,
            pltpu.SemaphoreType.DMA,
            pltpu.SemaphoreType.DMA,
        ],
        compiler_params=pltpu.CompilerParams(
            collective_id=0, has_side_effects=True, vmem_limit_bytes=48 * 1024 * 1024
        ),
        name="transform",
    )(wave_map, brackets, lev_weight, spectral, legendre)


def turn(product, points):
    inverse = 1.0 / points
    rest = product - jnp.floor(product * inverse + 0.5) * points
    x = rest * (math.pi * inverse)
    y = x * x
    sine = x * (
        1.0
        + y * (-1.0 / 6 + y * (1.0 / 120 + y * (-1.0 / 5040 + y * (1.0 / 362880 - y * (1.0 / 39916800)))))
    )
    cosine = 1.0 + y * (
        -0.5
        + y * (1.0 / 24 + y * (-1.0 / 720 + y * (1.0 / 40320 + y * (-1.0 / 3628800 + y * (1.0 / 479001600)))))
    )
    return 1.0 - 2.0 * (sine * sine), 2.0 * (sine * cosine)


def halves(x):
    high = x.astype(jnp.bfloat16)
    return high, (x - high.astype(jnp.float32)).astype(jnp.bfloat16)


def synthesis_kernel(
    points_ref, recv_ref, orders_ref, sign_ref, out_ref,
    coef, re_hi, re_lo, im_hi, im_lo, fine_c, fine_s, coarse_c, coarse_s, cand,
):
    count = points_ref[0]
    points = count.astype(jnp.float32)
    lane_block = lax.broadcasted_iota(jnp.int32, (8, LANES), 1) // COLS
    bits = [((lane_block >> t) & 1) == 1 for t in range(3)]
    for w in range(WAVES):
        for i0 in range(0, GROUPS, 8):
            keep = min(8, GROUPS - i0)
            held = [recv_ref[w * LEVS + p, i0 : i0 + 8, :] for p in range(LEVS)]
            for t in range(3):
                held = [jnp.where(bits[t], held[(x + (1 << t)) % 8], held[x]) for x in range(8)]
            for b in range(8):
                moved = held[-b % 8]
                if b:
                    moved = pltpu.roll(moved, LANES - COLS * b, 1)
                coef[b, w * GROUPS + i0 : w * GROUPS + i0 + keep, :] = moved[:keep]
    span = WAVES * GROUPS
    for u in range(4):
        at = slice(u * span, (u + 1) * span)
        sign = sign_ref[at, :]
        for part, (high_ref, low_ref) in enumerate(((re_hi, re_lo), (im_hi, im_lo))):
            plain = coef[2 * u + part]
            for side, value in enumerate((plain, plain * sign)):
                high, low = halves(value)
                high_ref[at, side * LANES : (side + 1) * LANES] = high
                low_ref[at, side * LANES : (side + 1) * LANES] = low

    orders = orders_ref[...]
    fine_k = lax.broadcasted_iota(jnp.int32, (KBLOCK, 1), 0).astype(jnp.float32)
    fine_c[...], fine_s[...] = turn(fine_k * orders, points)
    coarse_k = lax.broadcasted_iota(jnp.int32, (16, 1), 0).astype(jnp.float32) * KBLOCK
    factor = jnp.where(orders == 0.0, 1.0, 2.0)
    factor = jnp.where(orders <= ((count - 1) // 2).astype(jnp.float32), factor, 0.0)
    whole_c, whole_s = turn(coarse_k * orders, points)
    coarse_c[...] = whole_c * factor
    coarse_s[...] = whole_s * factor

    row = lax.broadcasted_iota(jnp.int32, (64, 4 * LANES), 0)
    col = lax.broadcasted_iota(jnp.int32, (64, 4 * LANES), 1)
    belongs = ((row >> 4) == (col >> 7)) & ((row & 7) == ((col >> 4) & 7)) & (((row >> 3) & 1) == ((col >> 3) & 1))
    gather = jnp.where(belongs, 0.125, 0.0).astype(jnp.bfloat16)
    flip_row = lax.broadcasted_iota(jnp.int32, (LANES, LANES), 0)
    flip_col = lax.broadcasted_iota(jnp.int32, (LANES, LANES), 1)
    flip = jnp.where(flip_row + flip_col == LANES - 1, 1.0, 0.0).astype(jnp.bfloat16)

    quarter = count // 4
    offsets = (0, 2 * quarter - (KSPAN - 1), 2 * quarter, 4 * quarter - (KSPAN - 1))
    shifts = [lax.rem(off + KSPAN, LANES) for off in offsets]
    heads = [(off + KSPAN) // LANES - KBLOCKS for off in offsets]

    def block(a, carry):
        cc, cs = coarse_c[pl.ds(a, 1), :], coarse_s[pl.ds(a, 1), :]
        fc, fs = fine_c[...], fine_s[...]
        dot = functools.partial(jnp.dot, preferred_element_type=jnp.float32)
        cos_hi, cos_lo = halves(fc * cc - fs * cs)
        real = dot(cos_hi, re_hi[...]) + dot(cos_lo, re_hi[...]) + dot(cos_hi, re_lo[...])
        sin_hi, sin_lo = halves(fs * cc + fc * cs)
        imag = dot(sin_hi, im_hi[...]) + dot(sin_lo, im_hi[...]) + dot(sin_hi, im_lo[...])
        p, q = real[:, :LANES], real[:, LANES:]
        r, s = imag[:, :LANES], imag[:, LANES:]
        values = jnp.concatenate([p - r, q + s, q - s, p + r], axis=1)
        sq_hi, sq_lo = halves(values * values)
        energy = lax.dot_general(gather, sq_hi, NT_DIMS, preferred_element_type=jnp.float32)
        energy = energy + lax.dot_general(gather, sq_lo, NT_DIMS, preferred_element_type=jnp.float32)
        e_hi, e_lo = halves(energy)
        back = dot(e_hi, flip) + dot(e_lo, flip)
        for x in range(4):
            tile = (back if x % 2 else energy)[16 * x : 16 * x + 16]
            place = (KBLOCKS - 1 - a) if x % 2 else a
            cand[x, place] = pltpu.roll(tile, shifts[x], 1) if x else tile
        return carry

    lax.fori_loop(0, KBLOCKS, block, 0)

    lane = lax.broadcasted_iota(jnp.int32, (16, LANES), 1)

    def finish(t, carry):
        place = t * LANES + lane
        picked = []
        for x in range(4):
            here = jnp.clip(t - heads[x], 0, KBLOCKS - 1)
            before = jnp.clip(t - heads[x] - 1, 0, KBLOCKS - 1)
            picked.append(jnp.where(lane >= shifts[x], cand[x, here], cand[x, before]))
        value = jnp.where(place < count, picked[3], 0.0)
        value = jnp.where(place <= 3 * quarter, picked[2], value)
        value = jnp.where(place <= 2 * quarter, picked[1], value)
        value = jnp.where(place <= quarter, picked[0], value)
        out_ref[pl.ds(t, 16, stride=ROWTILES), :] = value
        return carry

    lax.fori_loop(0, TILES, finish, 0)
    for t in range(TILES, ROWTILES):
        out_ref[pl.ds(t, 16, stride=ROWTILES), :] = jnp.zeros((16, LANES), jnp.float32)


def synthesis(points, recv, orders, sign):
    vmem = pl.BlockSpec(memory_space=pltpu.VMEM)
    return pl.pallas_call(
        synthesis_kernel,
        out_shape=jax.ShapeDtypeStruct((16 * ROWTILES, LANES), jnp.float32),
        in_specs=[pl.BlockSpec(memory_space=pltpu.SMEM), vmem, vmem, vmem],
        out_specs=vmem,
        scratch_shapes=[
            pltpu.VMEM((8, WAVES * GROUPS, LANES), jnp.float32),
            pltpu.VMEM((M, 2 * LANES), jnp.bfloat16),
            pltpu.VMEM((M, 2 * LANES), jnp.bfloat16),
            pltpu.VMEM((M, 2 * LANES), jnp.bfloat16),
            pltpu.VMEM((M, 2 * LANES), jnp.bfloat16),
            pltpu.VMEM((KBLOCK, M), jnp.float32),
            pltpu.VMEM((KBLOCK, M), jnp.float32),
            pltpu.VMEM((16, M), jnp.float32),
            pltpu.VMEM((16, M), jnp.float32),
            pltpu.VMEM((4, KBLOCKS, 16, LANES), jnp.float32),
        ],
        compiler_params=pltpu.CompilerParams(vmem_limit_bytes=48 * 1024 * 1024),
        name="synthesis",
    )(points, recv, orders, sign)


def back_kernel(points_ref, energy_ref, clim_ref, out_ref, got, send_sem, recv_sem, own_sem):
    wave, lev = lax.axis_index("wave"), lax.axis_index("lev")
    half, base = wave // 8, lax.rem(wave, 8)
    member = half * LEVS + lev
    barrier = pltpu.get_barrier_semaphore()

    def device(k):
        return base + 8 * (k // LEVS), lax.rem(k, LEVS)

    def greet(d, carry):
        pl.semaphore_signal(barrier, inc=1, device_id=device(lax.rem(member + d, 16)), device_id_type=MESH)
        return carry

    lax.fori_loop(1, 16, greet, 0)
    pl.semaphore_wait(barrier, 15)

    def rows(k):
        return pl.ds(pl.multiple_of(k * ROWTILES, 8), ROWTILES)

    def push(d, carry):
        k = lax.rem(member + d, 16)
        pltpu.make_async_remote_copy(
            src_ref=energy_ref.at[rows(k)],
            dst_ref=got.at[rows(member)],
            send_sem=send_sem,
            recv_sem=recv_sem,
            device_id=device(k),
            device_id_type=MESH,
        ).start()
        return carry

    lax.fori_loop(1, 16, push, 0)
    mine = pltpu.make_async_copy(energy_ref.at[rows(member)], got.at[rows(member)], own_sem)
    mine.start()
    mine.wait()
    part = pl.ds(0, 15 * ROWTILES)
    pltpu.make_async_copy(energy_ref.at[part], energy_ref.at[part], send_sem).wait()
    pltpu.make_async_copy(got.at[part], got.at[part], recv_sem).wait()

    row = lax.broadcasted_iota(jnp.int32, (16, LANES), 0)
    lane = lax.broadcasted_iota(jnp.int32, (16, LANES), 1)
    count = jnp.zeros((16, LANES), jnp.int32)
    for r in range(16):
        count = jnp.where(row == r, points_ref[base * 16 + r], count)
    for t in range(TILES):
        at = slice(t * LANES, (t + 1) * LANES)
        value = got[pl.ds(t, 16, stride=ROWTILES), :] - clim_ref[0, :, at]
        out_ref[0, :, at] = jnp.where(lane + t * LANES < count, value, 0.0)


def back(row_points, energy, climatology):
    vmem = pl.BlockSpec(memory_space=pltpu.VMEM)
    return pl.pallas_call(
        back_kernel,
        out_shape=jax.ShapeDtypeStruct((1, 16, ROWPAD), jnp.float32),
        in_specs=[pl.BlockSpec(memory_space=pltpu.SMEM), vmem, vmem],
        out_specs=vmem,
        scratch_shapes=[
            pltpu.VMEM((16 * ROWTILES, LANES), jnp.float32),
            pltpu.SemaphoreType.DMA,
            pltpu.SemaphoreType.DMA,
            pltpu.SemaphoreType.DMA,
        ],
        compiler_params=pltpu.CompilerParams(
            collective_id=1, has_side_effects=True, vmem_limit_bytes=32 * 1024 * 1024
        ),
        name="back",
    )(row_points, energy, climatology)


def local(spectral, legendre, wave_map, row_points, brackets, lev_weight, climatology):
    wave, lev = lax.axis_index("wave"), lax.axis_index("lev")
    recv = transform(wave_map, brackets, lev_weight, spectral, legendre)
    ordered = jnp.transpose(wave_map.reshape(WAVES, GROUPS, 4), (2, 0, 1))
    orders = ordered.reshape(1, M).astype(jnp.float32)
    sign = (1 - 2 * (ordered & 1)).astype(jnp.float32).reshape(M, 1)
    points = lax.dynamic_slice_in_dim(row_points, pair_of(wave, lev), 1, 0)
    energy = synthesis(points, recv, orders, sign)
    return back(row_points, energy, climatology)


def solution(mesh):
    placed = (
        P("wave", "lev", None),
        P("wave", None, None),
        P(),
        P(),
        P(),
        P(),
        P("lev", "wave", None),
    )
    return jax.shard_map(
        local, mesh=mesh, in_specs=placed, out_specs=P("lev", "wave", None), check_vma=False
    )
```

```python
import functools
import math

import jax
import jax.numpy as jnp
from jax import lax
from jax.experimental import pallas as pl
from jax.experimental.pallas import tpu as pltpu
from jax.sharding import PartitionSpec as P

MESH = pl.DeviceIdType.MESH

M = 1280
NT = 1280
LEV_DEV = 4
COLS = 16
HALF = 128
ROWPAD = 5248
LANES = 128

WAVES = 16
LEVS = 8
DEVICES = WAVES * LEVS
SLOTS = M // WAVES
STEP_SLOTS = 16
STEPS = SLOTS // STEP_SLOTS
STEP_ROWS = STEP_SLOTS * 2 * COLS
PER_SLOT = 2 * COLS
FIRST_ROWS, LAST_ROWS = 16, 8
PACK = FIRST_ROWS + LAST_ROWS
GROUPS = SLOTS // 4
FIRST = WAVES * 64
LAST = WAVES * 16
STRIDE = 37

KBLOCK = 128
KBLOCKS = 11
KSPAN = KBLOCK * KBLOCKS
KWIDE = 352
TILES = ROWPAD // LANES
ROWTILES = 48

NT_DIMS = (((1,), (1,)), ((), ()))


def pair_of(wave, lev):
    return (wave % 8) * 16 + (wave // 8) * 8 + lev


def turn(product, points):
    inverse = 1.0 / points
    rest = product - jnp.floor(product * inverse + 0.5) * points
    x = rest * (math.pi * inverse)
    y = x * x
    sine = x * (
        1.0
        + y * (-1.0 / 6 + y * (1.0 / 120 + y * (-1.0 / 5040 + y * (1.0 / 362880 - y * (1.0 / 39916800)))))
    )
    cosine = 1.0 + y * (
        -0.5
        + y * (1.0 / 24 + y * (-1.0 / 720 + y * (1.0 / 40320 + y * (-1.0 / 3628800 + y * (1.0 / 479001600)))))
    )
    return 1.0 - 2.0 * (sine * sine), 2.0 * (sine * cosine)


def halves(x):
    high = x.astype(jnp.bfloat16)
    return high, (x - high.astype(jnp.float32)).astype(jnp.bfloat16)


def dot(a, b):
    return jnp.dot(a, b, preferred_element_type=jnp.float32)


def kernel(
    waves_ref, brackets_ref, weight_ref, points_ref, orders_ref, spec_ref, leg_ref, out_ref,
    mixed, first, other, send, recv, coef, sign, re_hi, re_lo, im_hi, im_lo,
    fine_c, fine_s, coarse_c, coarse_s, cos_hi, cos_lo, sin_hi, sin_lo, acc, sq_hi, sq_lo, cand, energy_out, got,
    near_send, near_recv, far_send, far_recv, own_sem, back_send, back_recv, ready,
):
    step = pl.program_id(0)
    wave, lev = lax.axis_index("wave"), lax.axis_index("lev")
    me = wave * LEVS + lev
    below = lax.rem(lev + LEVS - 1, LEVS)
    barrier = pltpu.get_barrier_semaphore()

    @pl.when(step == 0)
    def _():
        for d in range(1, LEVS):
            pl.semaphore_signal(
                barrier, inc=1, device_id=(wave, lax.rem(lev + d, LEVS)), device_id_type=MESH
            )
        for d in range(1, WAVES):
            pl.semaphore_signal(
                barrier, inc=1, device_id=(lax.rem(wave + d, WAVES), lev), device_id_type=MESH
            )

    lower = brackets_ref[lev] - lev * LEV_DEV
    weight = weight_ref[lev]
    inside = lower < LEV_DEV - 1
    gain = jnp.where(inside, 0.0, 1.0 - weight)
    level_weight = [
        jnp.where(lower == v, weight, 0.0) + jnp.where(lower + 1 == v, 1.0 - weight, 0.0) for v in range(LEV_DEV)
    ]

    degree = lax.broadcasted_iota(jnp.int32, (1, NT), 1)
    for i in range(STEP_SLOTS):
        order = waves_ref[wave * SLOTS + step * STEP_SLOTS + i]
        kept = jnp.where(degree >= order, 1.0, 0.0)
        signed = kept * (1 - 2 * ((degree + order) & 1)).astype(jnp.float32)
        kept, signed = kept.astype(jnp.bfloat16), signed.astype(jnp.bfloat16)
        coeffs = spec_ref[i]
        both = jnp.concatenate([coeffs * kept, coeffs * signed], axis=0)
        sums = lax.dot_general(both, leg_ref[i], NT_DIMS, preferred_element_type=jnp.float32)
        base = step * STEP_ROWS + i * PER_SLOT
        for hemi in range(2):
            own = [sums[(LEV_DEV * hemi + v) * COLS : (LEV_DEV * hemi + v + 1) * COLS] for v in range(LEV_DEV)]
            at = pl.ds(pl.multiple_of(base + hemi * COLS, COLS), COLS)
            total = own[0] * level_weight[0]
            for v in range(1, LEV_DEV):
                total = total + own[v] * level_weight[v]
            mixed[at, :] = total
            first[at, :] = own[0]

    def near_copy(t):
        rows = pl.ds(pl.multiple_of(t * STEP_ROWS, STEP_ROWS), STEP_ROWS)
        return pltpu.make_async_remote_copy(
            src_ref=first.at[rows],
            dst_ref=other.at[rows],
            send_sem=near_send.at[t],
            recv_sem=near_recv.at[t],
            device_id=(wave, below),
            device_id_type=MESH,
        )

    @pl.when(step == 0)
    def _():
        pl.semaphore_wait(barrier, LEVS + WAVES - 2)
        for d in range(1, LEVS):
            pl.semaphore_signal(
                ready, inc=1, device_id=(wave, lax.rem(lev + d, LEVS)), device_id_type=MESH
            )

    near_copy(step).start()

    def assemble(g, slot_of):
        pieces = []
        for c in range(8):
            b = lax.rem(c - lev + 8, 8)
            base = slot_of(b // 2) * PER_SLOT + lax.rem(b, 2)
            for hemi in range(2):
                at = pl.ds(base + hemi * COLS, 8, stride=2)
                pieces.append(mixed[at, :] + gain * other[at, :])
        block = jnp.concatenate(pieces, axis=0)
        send[pl.ds(g, HALF, stride=PACK), :] = block.T

    def assemble_pair(tau):
        near_copy(2 * tau).wait_recv()
        near_copy(2 * tau + 1).wait_recv()

        def one(r, carry):
            assemble(8 * tau + r, lambda u: 32 * tau + 8 * u + r)
            return carry

        lax.fori_loop(0, 8, one, 0)

    def far_copy(d, start, count, part):
        target = lax.rem(me + STRIDE * d, DEVICES)
        to_wave, to_lev = target // LEVS, lax.rem(target, LEVS)
        at = pl.multiple_of(pair_of(to_wave, to_lev) * PACK + start, 8)
        return pltpu.make_async_remote_copy(
            src_ref=send.at[pl.ds(at, count)],
            dst_ref=recv.at[me, pl.ds(start, count)],
            send_sem=far_send.at[part],
            recv_sem=far_recv.at[part],
            device_id=(to_wave, to_lev),
            device_id_type=MESH,
        )

    def push(start, count, part):
        def one(d, carry):
            far_copy(d, start, count, part).start()
            return carry

        lax.fori_loop(1, DEVICES, one, 0)
        at = pl.multiple_of(pair_of(wave, lev) * PACK + start, 8)
        pltpu.make_async_copy(
            send.at[pl.ds(at, count)], recv.at[me, pl.ds(start, count)], own_sem.at[part]
        ).start()

    def arrive(start, count, part):
        mine = recv.at[me, pl.ds(start, count)]
        pltpu.make_async_copy(mine, mine, own_sem.at[part]).wait()
        block = recv.at[pl.ds(0, DEVICES - 1), pl.ds(start, count)]
        pltpu.make_async_copy(block, block, far_recv.at[part]).wait()

    def left(start, count, part):
        block = recv.at[pl.ds(0, DEVICES - 1), pl.ds(start, count)]
        pltpu.make_async_copy(block, block, far_send.at[part]).wait()

    @pl.when(step == 0)
    def _():
        for g in range(GROUPS, PACK):
            send[pl.ds(g, HALF, stride=PACK), :] = jnp.zeros((HALF, LANES), jnp.float32)

    @pl.when(step == 3)
    def _():
        assemble_pair(0)

    @pl.when(step == STEPS - 1)
    def _():
        assemble_pair(1)
        pl.semaphore_wait(ready, LEVS - 1)
        push(0, FIRST_ROWS, 0)

        count = points_ref[pair_of(wave, lev)]
        points = count.astype(jnp.float32)
        natural = orders_ref[...].reshape(1, M).astype(jnp.float32)
        pieces = [natural[:, w * SLOTS : w * SLOTS + 64] for w in range(WAVES)]
        pieces += [natural[:, w * SLOTS + 64 : (w + 1) * SLOTS] for w in range(WAVES)]
        orders = jnp.concatenate(pieces, axis=1)
        fine_k = lax.broadcasted_iota(jnp.int32, (KBLOCK, 1), 0).astype(jnp.float32)
        fine_c[...], fine_s[...] = turn(fine_k * orders, points)
        coarse_k = lax.broadcasted_iota(jnp.int32, (16, 1), 0).astype(jnp.float32) * KBLOCK
        factor = jnp.where(orders == 0.0, 1.0, 2.0)
        factor = jnp.where(orders <= ((count - 1) // 2).astype(jnp.float32), factor, 0.0)
        whole_c, whole_s = turn(coarse_k * orders, points)
        coarse_c[...] = whole_c * factor
        coarse_s[...] = whole_s * factor

        near_copy(STEPS - 1).wait_recv()

        def one(q, carry):
            assemble(16 + q, lambda u: 64 + 4 * u + q)
            return carry

        lax.fori_loop(0, 4, one, 0)
        push(FIRST_ROWS, LAST_ROWS, 1)

        def basis(a, carry):
            cc, cs = coarse_c[pl.ds(a, 1), :], coarse_s[pl.ds(a, 1), :]
            at = pl.ds(pl.multiple_of(a * KBLOCK, KBLOCK), KBLOCK)
            for lanes in range(0, M, 256):
                part = slice(lanes, lanes + 256)
                fc, fs = fine_c[:, part], fine_s[:, part]
                c, s = cc[:, part], cs[:, part]
                cos_hi[at, part], cos_lo[at, part] = halves(fc * c - fs * s)
                sin_hi[at, part], sin_lo[at, part] = halves(fs * c + fc * s)
            return carry

        lax.fori_loop(0, KBLOCKS, basis, 0)
        parity = (1 - 2 * (orders.astype(jnp.int32) & 1)).astype(jnp.float32)
        for i in range(0, M, LANES):
            wide = jnp.broadcast_to(parity[:, i : i + LANES], (LANES, LANES))
            sign[i : i + LANES, :] = wide.T.astype(jnp.bfloat16)

        lane_block = lax.broadcasted_iota(jnp.int32, (8, LANES), 1) // COLS
        bits = [((lane_block >> t) & 1) == 1 for t in range(3)]

        def spread(w, i0):
            held = [recv[w * LEVS + p, i0 : i0 + 8, :] for p in range(LEVS)]
            for t in range(3):
                held = [jnp.where(bits[t], held[(x + (1 << t)) % 8], held[x]) for x in range(8)]
            for b in range(8):
                moved = held[-b % 8]
                if b:
                    moved = pltpu.roll(moved, LANES - COLS * b, 1)
                u, part = b // 2, b % 2
                if i0 < FIRST_ROWS:
                    base = w * 64 + 4 * i0 + 8 * u
                    coef[part, base : base + 8, :] = moved
                else:
                    base = FIRST + w * 16 + 4 * u
                    coef[part, base : base + 4, :] = moved[:4]

        def split(low, high):
            at = slice(low, high)
            flip_sign = sign[at, :]
            for part, (high_ref, low_ref) in enumerate(((re_hi, re_lo), (im_hi, im_lo))):
                for ref, value in zip((high_ref, low_ref), halves(coef[part, at, :])):
                    ref[at, :LANES] = value
                    ref[at, LANES:] = value * flip_sign

        def partial(rows, cols):
            real = dot(cos_hi[rows, cols], re_hi[cols, :]) + dot(cos_lo[rows, cols], re_hi[cols, :])
            real = real + dot(cos_hi[rows, cols], re_lo[cols, :])
            imag = dot(sin_hi[rows, cols], im_hi[cols, :]) + dot(sin_lo[rows, cols], im_hi[cols, :])
            imag = imag + dot(sin_hi[rows, cols], im_lo[cols, :])
            return real, imag

        arrive(0, FIRST_ROWS, 0)
        for w in range(WAVES):
            for i0 in range(0, FIRST_ROWS, 8):
                spread(w, i0)
        split(0, FIRST)

        def early(a, carry):
            rows = pl.ds(pl.multiple_of(a * KWIDE, 32), KWIDE)
            acc[rows, : 2 * LANES], acc[rows, 2 * LANES :] = partial(rows, slice(0, FIRST))
            return carry

        lax.fori_loop(0, KSPAN // KWIDE, early, 0)

        row = lax.broadcasted_iota(jnp.int32, (64, 4 * LANES), 0)
        col = lax.broadcasted_iota(jnp.int32, (64, 4 * LANES), 1)
        belongs = (
            ((row >> 4) == (col >> 7)) & ((row & 7) == ((col >> 4) & 7)) & (((row >> 3) & 1) == ((col >> 3) & 1))
        )
        gather = jnp.where(belongs, 0.125, 0.0).astype(jnp.bfloat16)
        flip_row = lax.broadcasted_iota(jnp.int32, (LANES, LANES), 0)
        flip_col = lax.broadcasted_iota(jnp.int32, (LANES, LANES), 1)
        flip = jnp.where(flip_row + flip_col == LANES - 1, 1.0, 0.0).astype(jnp.bfloat16)
        quarter = count // 4
        offsets = (0, 2 * quarter - (KSPAN - 1), 2 * quarter, 4 * quarter - (KSPAN - 1))
        shifts = [lax.rem(off + KSPAN, LANES) for off in offsets]
        heads = [(off + KSPAN) // LANES - KBLOCKS for off in offsets]
        shift_bits = [[((shift >> t) & 1) == 1 for t in range(7)] for shift in shifts]

        def turned(tile, x):
            for t in range(7):
                tile = jnp.where(shift_bits[x][t], pltpu.roll(tile, 1 << t, 1), tile)
            return tile


        arrive(FIRST_ROWS, LAST_ROWS, 1)
        for w in range(WAVES):
            spread(w, FIRST_ROWS)
        split(FIRST, M)

        def late(a, carry):
            rows = pl.ds(pl.multiple_of(a * KWIDE, 32), KWIDE)
            real, imag = partial(rows, slice(FIRST, M))
            real, imag = real + acc[rows, : 2 * LANES], imag + acc[rows, 2 * LANES :]
            p, q = real[:, :LANES], real[:, LANES:]
            r, s = imag[:, :LANES], imag[:, LANES:]
            for x, value in enumerate((p - r, q + s, q - s, p + r)):
                part = slice(x * LANES, (x + 1) * LANES)
                sq_hi[rows, part], sq_lo[rows, part] = halves(value * value)
            return carry

        lax.fori_loop(0, KSPAN // KWIDE, late, 0)
        energy = lax.dot_general(gather, sq_hi[...], NT_DIMS, preferred_element_type=jnp.float32)
        energy = energy + lax.dot_general(gather, sq_lo[...], NT_DIMS, preferred_element_type=jnp.float32)
        tiles = [energy[:, a * LANES : (a + 1) * LANES] for a in range(KBLOCKS)]
        for x in (0, 2):
            for a in range(KBLOCKS):
                tile = tiles[a][16 * x : 16 * x + 16]
                cand[x, a] = turned(tile, x) if x else tile
        ahead = jnp.concatenate([tile[16 * x : 16 * x + 16] for x in (1, 3) for tile in reversed(tiles)], axis=0)
        e_hi, e_lo = halves(ahead)
        back = dot(e_hi, flip) + dot(e_lo, flip)
        for x in (1, 3):
            for a in range(KBLOCKS):
                at = (x // 2 * KBLOCKS + a) * 16
                cand[x, a] = turned(back[at : at + 16], x)

        lane = lax.broadcasted_iota(jnp.int32, (16, LANES), 1)

        for t in range(TILES):
            place = t * LANES + lane
            picked = []
            for x in range(4):
                here = jnp.clip(t - heads[x], 0, KBLOCKS - 1)
                before = jnp.clip(t - heads[x] - 1, 0, KBLOCKS - 1)
                picked.append(jnp.where(lane >= shifts[x], cand[x, here], cand[x, before]))
            value = jnp.where(place < count, picked[3], -1.0)
            value = jnp.where(place <= 3 * quarter, picked[2], value)
            value = jnp.where(place <= 2 * quarter, picked[1], value)
            value = jnp.where(place <= quarter, picked[0], value)
            energy_out[pl.ds(t, 16, stride=ROWTILES), :] = value
        for t in range(TILES, ROWTILES):
            energy_out[pl.ds(t, 16, stride=ROWTILES), :] = jnp.zeros((16, LANES), jnp.float32)

        half, band = wave // 8, lax.rem(wave, 8)
        member = half * LEVS + lev

        def rows_of(k):
            return pl.ds(pl.multiple_of(k * ROWTILES, 8), ROWTILES)

        def send_back(d, carry):
            k = lax.rem(member + d, 16)
            pltpu.make_async_remote_copy(
                src_ref=energy_out.at[rows_of(k)],
                dst_ref=got.at[rows_of(member)],
                send_sem=back_send,
                recv_sem=back_recv,
                device_id=(band + 8 * (k // LEVS), lax.rem(k, LEVS)),
                device_id_type=MESH,
            ).start()
            return carry

        lax.fori_loop(1, 16, send_back, 0)
        mine = pltpu.make_async_copy(energy_out.at[rows_of(member)], got.at[rows_of(member)], own_sem.at[0])
        mine.start()
        mine.wait()
        for t in range(STEPS):
            near_copy(t).wait_send()
        left(0, FIRST_ROWS, 0)
        left(FIRST_ROWS, LAST_ROWS, 1)
        part = pl.ds(0, 15 * ROWTILES)
        pltpu.make_async_copy(energy_out.at[part], energy_out.at[part], back_send).wait()
        pltpu.make_async_copy(got.at[part], got.at[part], back_recv).wait()

        for t in range(TILES):
            out_ref[0, :, t * LANES : (t + 1) * LANES] = got[pl.ds(t, 16, stride=ROWTILES), :]


def local(spectral, legendre, wave_map, row_points, brackets, lev_weight, climatology):
    smem = pl.BlockSpec(memory_space=pltpu.SMEM)
    vmem = pl.BlockSpec(memory_space=pltpu.VMEM)
    rows = SLOTS * PER_SLOT
    f32, bf16, dma = jnp.float32, jnp.bfloat16, pltpu.SemaphoreType.DMA
    energy = pl.pallas_call(
        kernel,
        grid=(STEPS,),
        out_shape=jax.ShapeDtypeStruct((1, 16, ROWPAD), f32),
        in_specs=[
            smem,
            smem,
            smem,
            smem,
            vmem,
            pl.BlockSpec((STEP_SLOTS, LEV_DEV * COLS, NT), lambda t: (t, 0, 0)),
            pl.BlockSpec((STEP_SLOTS, HALF, NT), lambda t: (t, 0, 0)),
        ],
        out_specs=vmem,
        scratch_shapes=[
            pltpu.VMEM((rows, HALF), f32),
            pltpu.VMEM((rows, HALF), f32),
            pltpu.VMEM((rows, HALF), f32),
            pltpu.VMEM((HALF * PACK, LANES), f32),
            pltpu.VMEM((DEVICES, PACK, LANES), f32),
            pltpu.VMEM((2, M, LANES), f32),
            pltpu.VMEM((M, LANES), bf16),
            pltpu.VMEM((M, 2 * LANES), bf16),
            pltpu.VMEM((M, 2 * LANES), bf16),
            pltpu.VMEM((M, 2 * LANES), bf16),
            pltpu.VMEM((M, 2 * LANES), bf16),
            pltpu.VMEM((KBLOCK, M), f32),
            pltpu.VMEM((KBLOCK, M), f32),
            pltpu.VMEM((16, M), f32),
            pltpu.VMEM((16, M), f32),
            pltpu.VMEM((KSPAN, M), bf16),
            pltpu.VMEM((KSPAN, M), bf16),
            pltpu.VMEM((KSPAN, M), bf16),
            pltpu.VMEM((KSPAN, M), bf16),
            pltpu.VMEM((KSPAN, 4 * LANES), f32),
            pltpu.VMEM((KSPAN, 4 * LANES), bf16),
            pltpu.VMEM((KSPAN, 4 * LANES), bf16),
            pltpu.VMEM((4, KBLOCKS, 16, LANES), f32),
            pltpu.VMEM((16 * ROWTILES, LANES), f32),
            pltpu.VMEM((16 * ROWTILES, LANES), f32),
            dma((STEPS,)),
            dma((STEPS,)),
            dma((2,)),
            dma((2,)),
            dma((2,)),
            dma,
            dma,
            pltpu.SemaphoreType.REGULAR,
        ],
        compiler_params=pltpu.CompilerParams(
            collective_id=0, has_side_effects=True, vmem_limit_bytes=60 * 1024 * 1024
        ),
        name="transform",
    )(wave_map, brackets, lev_weight, row_points, wave_map, spectral, legendre)
    return jnp.where(energy < 0.0, 0.0, energy - climatology)


def solution(mesh):
    placed = (
        P("wave", "lev", None),
        P("wave", None, None),
        P(),
        P(),
        P(),
        P(),
        P("lev", "wave", None),
    )
    return jax.shard_map(
        local, mesh=mesh, in_specs=placed, out_specs=P("lev", "wave", None), check_vma=False
    )
```

```python
import functools
import math

import jax
import jax.numpy as jnp
from jax import lax
from jax.experimental import pallas as pl
from jax.experimental.pallas import tpu as pltpu
from jax.sharding import PartitionSpec as P

MESH = pl.DeviceIdType.MESH

M = 1280
NT = 1280
LEV_DEV = 4
COLS = 16
HALF = 128
ROWPAD = 5248
LANES = 128

WAVES = 16
LEVS = 8
DEVICES = WAVES * LEVS
SLOTS = M // WAVES
STEP_SLOTS = 8
STEPS = SLOTS // STEP_SLOTS
STEP_ROWS = STEP_SLOTS * 2 * COLS
PER_SLOT = 2 * COLS
GROUPS = SLOTS // 4
PARTS = ((0, 32, 8), (32, 32, 8), (64, 16, 4))
PACK = 2 * GROUPS
PART_AT = (0, 16, 32)
PART_SLOT = (0, WAVES * 32, WAVES * 64)
BUFFERS = 4
STRIDE = 37

KBLOCK = 128
KBLOCKS = 11
KSPAN = KBLOCK * KBLOCKS
KWIDE = 352
TILES = ROWPAD // LANES
ROWTILES = 48

NT_DIMS = (((1,), (1,)), ((), ()))


def pair_of(wave, lev):
    return (wave % 8) * 16 + (wave // 8) * 8 + lev


def turn(product, points):
    inverse = 1.0 / points
    rest = product - jnp.floor(product * inverse + 0.5) * points
    x = rest * (math.pi * inverse)
    y = x * x
    sine = x * (
        1.0
        + y * (-1.0 / 6 + y * (1.0 / 120 + y * (-1.0 / 5040 + y * (1.0 / 362880 - y * (1.0 / 39916800)))))
    )
    cosine = 1.0 + y * (
        -0.5
        + y * (1.0 / 24 + y * (-1.0 / 720 + y * (1.0 / 40320 + y * (-1.0 / 3628800 + y * (1.0 / 479001600)))))
    )
    return 1.0 - 2.0 * (sine * sine), 2.0 * (sine * cosine)


def halves(x):
    high = x.astype(jnp.bfloat16)
    return high, (x - high.astype(jnp.float32)).astype(jnp.bfloat16)


def dot(a, b):
    return jnp.dot(a, b, preferred_element_type=jnp.float32)


def kernel(
    waves_ref, brackets_ref, weight_ref, points_ref, orders_ref, spec_hbm, leg_hbm, out_ref,
    spec_ref, leg_ref, load_sem, mixed, first, other, send, recv, coef, sign, re_hi, re_lo, im_hi, im_lo,
    fine_c, fine_s, coarse_c, coarse_s, cos_hi, cos_lo, sin_hi, sin_lo, acc, sq_hi, sq_lo, cand, energy_out, got,
    near_send, near_recv, far_send, far_recv, own_sem, back_send, back_recv, ready,
):
    step = pl.program_id(0)
    wave, lev = lax.axis_index("wave"), lax.axis_index("lev")
    me = wave * LEVS + lev
    barrier = pltpu.get_barrier_semaphore()

    def loads(t):
        slot = lax.rem(t, BUFFERS)
        at = pl.ds(pl.multiple_of(t * STEP_SLOTS, STEP_SLOTS), STEP_SLOTS)
        return (
            pltpu.make_async_copy(spec_hbm.at[at], spec_ref.at[slot], load_sem.at[0, slot]),
            pltpu.make_async_copy(leg_hbm.at[at], leg_ref.at[slot], load_sem.at[1, slot]),
        )

    @pl.when(step == 0)
    def _():
        for t in range(BUFFERS - 1):
            for load in loads(t):
                load.start()

    @pl.when(step + BUFFERS - 1 < STEPS)
    def _():
        for load in loads(step + BUFFERS - 1):
            load.start()

    @pl.when(step == 0)
    def _():
        for d in range(1, LEVS):
            pl.semaphore_signal(
                barrier, inc=1, device_id=(wave, lax.rem(lev + d, LEVS)), device_id_type=MESH
            )
        for d in range(1, WAVES):
            pl.semaphore_signal(
                barrier, inc=1, device_id=(lax.rem(wave + d, WAVES), lev), device_id_type=MESH
            )

    lower = brackets_ref[lev] - lev * LEV_DEV
    weight = weight_ref[lev]
    gain = jnp.where(lower == LEV_DEV - 1, 1.0 - weight, 0.0)
    odd = (lev & 1) == 1
    even = (lev & 1) == 0
    prior = jnp.maximum(lev - 1, 0)
    prior_last = (brackets_ref[prior] == prior * LEV_DEV + LEV_DEV - 1) & (lev > 0)
    prior_gain = jnp.where(prior_last, 1.0 - weight_ref[prior], 0.0)
    level_weight = [
        jnp.where(lower == v, weight, 0.0) + jnp.where(lower + 1 == v, 1.0 - weight, 0.0) for v in range(LEV_DEV)
    ]

    def near_copy(t):
        rows = pl.ds(pl.multiple_of(t * STEP_ROWS, STEP_ROWS), STEP_ROWS)
        return pltpu.make_async_remote_copy(
            src_ref=first.at[rows],
            dst_ref=other.at[rows],
            send_sem=near_send.at[t],
            recv_sem=near_recv.at[t],
            device_id=(wave, lev ^ 1),
            device_id_type=MESH,
        )

    def assemble(g, slot_of, turn_by, value, row):
        pieces = []
        for c in range(8):
            b = (c - turn_by + 8) & 7
            base = slot_of(b >> 1) * PER_SLOT + (b & 1)
            for hemi in range(2):
                pieces.append(value(pl.ds(base + hemi * COLS, 8, stride=2)))
        send[pl.ds(row, HALF, stride=PACK), :] = jnp.concatenate(pieces, axis=0).T

    def assemble_part(part):
        begin, slots, count = PARTS[part]
        at = PART_AT[part]

        @pl.when(even)
        def _():
            for t in range(begin // STEP_SLOTS, (begin + slots) // STEP_SLOTS):
                near_copy(t).wait_recv()

            def one(r, carry):
                slot_of = lambda u: begin + count * u + r
                assemble(r, slot_of, lev, lambda rows: mixed[rows, :] + gain * other[rows, :], at + r)
                assemble(r, slot_of, lev - 1, lambda rows: prior_gain * first[rows, :], at + count + r)
                return carry

            lax.fori_loop(0, count, one, 0)

        @pl.when(odd)
        def _():
            def one(r, carry):
                assemble(r, lambda u: begin + count * u + r, lev, lambda rows: mixed[rows, :], at + r)
                return carry

            lax.fori_loop(0, count, one, 0)

    def push(part):
        at, count = PART_AT[part], PARTS[part][2]

        def send_rows(height):
            def one(i, carry):
                d = (STRIDE * i) & (DEVICES - 1)
                dw, dl = d >> 3, d & 7
                pair = pair_of(wave, lev) ^ (((dw & 7) << 4) | ((dw >> 3) << 3) | dl)
                pltpu.make_async_remote_copy(
                    src_ref=send.at[pl.ds(pl.multiple_of(pair * PACK + at, 8), height)],
                    dst_ref=recv.at[pl.ds(pl.multiple_of(me * PACK + at, 8), height)],
                    send_sem=far_send.at[part],
                    recv_sem=far_recv.at[part],
                    device_id=(wave ^ dw, lev ^ dl),
                    device_id_type=MESH,
                ).start()
                return carry

            lax.fori_loop(1, DEVICES, one, 0)

        if count == 8:
            pl.when(even)(lambda: send_rows(16))
            pl.when(odd)(lambda: send_rows(8))
        else:
            send_rows(8)
        mine = pl.multiple_of(pair_of(wave, lev) * PACK + at, 8)
        pltpu.make_async_copy(
            send.at[pl.ds(mine, 2 * count)],
            recv.at[pl.ds(pl.multiple_of(me * PACK + at, 8), 2 * count)],
            own_sem.at[part],
        ).start()

    def all_of(part, sem, even_rows, odd_rows):
        def wait(rows):
            block = recv.at[pl.ds(0, rows)]
            pltpu.make_async_copy(block, block, sem.at[part]).wait()

        if PARTS[part][2] == 8:
            pl.when(even)(lambda: wait(even_rows))
            pl.when(odd)(lambda: wait(odd_rows))
        else:
            wait((DEVICES - 1) * 8)

    def arrive(part):
        mine = recv.at[pl.ds(0, 2 * PARTS[part][2])]
        pltpu.make_async_copy(mine, mine, own_sem.at[part]).wait()
        others = DEVICES // 2
        all_of(part, far_recv, (others - 1) * 16 + others * 8, others * 16 + (others - 1) * 8)

    def left(part):
        all_of(part, far_send, (DEVICES - 1) * 16, (DEVICES - 1) * 8)

    @pl.when(step == 1)
    def _():
        pl.semaphore_wait(barrier, LEVS + WAVES - 2)
        for d in range(1, LEVS):
            pl.semaphore_signal(
                ready, inc=1, device_id=(wave, lax.rem(lev + d, LEVS)), device_id_type=MESH
            )

        @pl.when(odd)
        def _():
            near_copy(0).start()

    @pl.when(step == 0)
    def _():
        for part in range(3):
            _, _, count = PARTS[part]
            for r in range(count):
                send[pl.ds(PART_AT[part] + count + r, HALF, stride=PACK), :] = jnp.zeros((HALF, LANES), jnp.float32)

    @pl.when(step == 4)
    def _():
        assemble_part(0)
        pl.semaphore_wait(ready, LEVS - 1)
        push(0)

    @pl.when(step == STEPS - 1)
    def _():
        assemble_part(1)
        push(1)

    for load in loads(step):
        load.wait()
    held_at = lax.rem(step, BUFFERS)
    degree = lax.broadcasted_iota(jnp.int32, (1, NT), 1)
    for i in range(STEP_SLOTS):
        order = waves_ref[wave * SLOTS + step * STEP_SLOTS + i]
        kept = jnp.where(degree >= order, 1.0, 0.0)
        signed = kept * (1 - 2 * ((degree + order) & 1)).astype(jnp.float32)
        kept, signed = kept.astype(jnp.bfloat16), signed.astype(jnp.bfloat16)
        coeffs = spec_ref[held_at, i]
        both = jnp.concatenate([coeffs * kept, coeffs * signed], axis=0)
        sums = lax.dot_general(both, leg_ref[held_at, i], NT_DIMS, preferred_element_type=jnp.float32)
        base = step * STEP_ROWS + i * PER_SLOT
        for hemi in range(2):
            own = [sums[(LEV_DEV * hemi + v) * COLS : (LEV_DEV * hemi + v + 1) * COLS] for v in range(LEV_DEV)]
            at = pl.ds(pl.multiple_of(base + hemi * COLS, COLS), COLS)
            total = own[0] * level_weight[0]
            for v in range(1, LEV_DEV):
                total = total + own[v] * level_weight[v]
            mixed[at, :] = total
            first[at, :] = own[0]

    @pl.when(odd & (step > 0))
    def _():
        near_copy(step).start()

    @pl.when(step == STEPS - 1)
    def _():
        assemble_part(2)
        push(2)

        count = points_ref[pair_of(wave, lev)]
        points = count.astype(jnp.float32)
        natural = orders_ref[...].reshape(1, M).astype(jnp.float32)
        pieces = []
        for begin, slots, _ in PARTS:
            pieces += [natural[:, w * SLOTS + begin : w * SLOTS + begin + slots] for w in range(WAVES)]
        orders = jnp.concatenate(pieces, axis=1)
        fine_k = lax.broadcasted_iota(jnp.int32, (KBLOCK, 1), 0).astype(jnp.float32)
        fine_c[...], fine_s[...] = turn(fine_k * orders, points)
        coarse_k = lax.broadcasted_iota(jnp.int32, (16, 1), 0).astype(jnp.float32) * KBLOCK
        factor = jnp.where(orders == 0.0, 1.0, 2.0)
        factor = jnp.where(orders <= ((count - 1) // 2).astype(jnp.float32), factor, 0.0)
        whole_c, whole_s = turn(coarse_k * orders, points)
        coarse_c[...] = whole_c * factor
        coarse_s[...] = whole_s * factor

        def basis(a, carry):
            cc, cs = coarse_c[pl.ds(a, 1), :], coarse_s[pl.ds(a, 1), :]
            at = pl.ds(pl.multiple_of(a * KBLOCK, KBLOCK), KBLOCK)
            for lanes in range(0, M, 256):
                part = slice(lanes, lanes + 256)
                fc, fs = fine_c[:, part], fine_s[:, part]
                c, s = cc[:, part], cs[:, part]
                cos_hi[at, part], cos_lo[at, part] = halves(fc * c - fs * s)
                sin_hi[at, part], sin_lo[at, part] = halves(fs * c + fc * s)
            return carry

        lax.fori_loop(0, KBLOCKS, basis, 0)
        parity = (1 - 2 * (orders.astype(jnp.int32) & 1)).astype(jnp.float32)
        for i in range(0, M, LANES):
            wide = jnp.broadcast_to(parity[:, i : i + LANES], (LANES, LANES))
            sign[i : i + LANES, :] = wide.T.astype(jnp.bfloat16)

        lane_block = lax.broadcasted_iota(jnp.int32, (8, LANES), 1) // COLS
        bits = [((lane_block >> t) & 1) == 1 for t in range(3)]

        def spread(w, part):
            _, slots, count = PARTS[part]
            at = [(w * LEVS + p) * PACK + PART_AT[part] for p in range(LEVS)]
            held = [recv[at[p] : at[p] + 8, :] for p in range(LEVS)]
            for p in range(1, LEVS - 1, 2):
                if count == 8:
                    held[p] = held[p] + recv[at[p + 1] + 8 : at[p + 1] + 16, :]
                else:
                    held[p] = held[p] + pltpu.roll(held[p + 1], 4, 0)
            for t in range(3):
                held = [jnp.where(bits[t], held[(x + (1 << t)) % 8], held[x]) for x in range(8)]
            for b in range(8):
                moved = held[-b % 8]
                if b:
                    moved = pltpu.roll(moved, LANES - COLS * b, 1)
                base = PART_SLOT[part] + w * slots + count * (b // 2)
                coef[b % 2, base : base + count, :] = moved[:count]

        def split(low, high):
            at = slice(low, high)
            flip_sign = sign[at, :]
            for part, (high_ref, low_ref) in enumerate(((re_hi, re_lo), (im_hi, im_lo))):
                for ref, value in zip((high_ref, low_ref), halves(coef[part, at, :])):
                    ref[at, :LANES] = value
                    ref[at, LANES:] = value * flip_sign

        def partial(rows, cols):
            real = dot(cos_hi[rows, cols], re_hi[cols, :]) + dot(cos_lo[rows, cols], re_hi[cols, :])
            real = real + dot(cos_hi[rows, cols], re_lo[cols, :])
            imag = dot(sin_hi[rows, cols], im_hi[cols, :]) + dot(sin_lo[rows, cols], im_hi[cols, :])
            imag = imag + dot(sin_hi[rows, cols], im_lo[cols, :])
            return real, imag

        def gathered(part):
            arrive(part)
            for w in range(WAVES):
                spread(w, part)
            begin = PART_SLOT[part]
            split(begin, begin + WAVES * PARTS[part][1])
            return slice(begin, begin + WAVES * PARTS[part][1])

        cols = gathered(0)

        def early(a, carry):
            rows = pl.ds(pl.multiple_of(a * KWIDE, 32), KWIDE)
            acc[rows, : 2 * LANES], acc[rows, 2 * LANES :] = partial(rows, cols)
            return carry

        lax.fori_loop(0, KSPAN // KWIDE, early, 0)
        cols_next = gathered(1)

        def second(a, carry):
            rows = pl.ds(pl.multiple_of(a * KWIDE, 32), KWIDE)
            real, imag = partial(rows, cols_next)
            acc[rows, : 2 * LANES] = acc[rows, : 2 * LANES] + real
            acc[rows, 2 * LANES :] = acc[rows, 2 * LANES :] + imag
            return carry

        lax.fori_loop(0, KSPAN // KWIDE, second, 0)

        row = lax.broadcasted_iota(jnp.int32, (64, 4 * LANES), 0)
        col = lax.broadcasted_iota(jnp.int32, (64, 4 * LANES), 1)
        belongs = (
            ((row >> 4) == (col >> 7)) & ((row & 7) == ((col >> 4) & 7)) & (((row >> 3) & 1) == ((col >> 3) & 1))
        )
        gather = jnp.where(belongs, 0.125, 0.0).astype(jnp.bfloat16)
        flip_row = lax.broadcasted_iota(jnp.int32, (LANES, LANES), 0)
        flip_col = lax.broadcasted_iota(jnp.int32, (LANES, LANES), 1)
        flip = jnp.where(flip_row + flip_col == LANES - 1, 1.0, 0.0).astype(jnp.bfloat16)
        quarter = count // 4
        offsets = (0, 2 * quarter - (KSPAN - 1), 2 * quarter, 4 * quarter - (KSPAN - 1))
        shifts = [lax.rem(off + KSPAN, LANES) for off in offsets]
        heads = [(off + KSPAN) // LANES - KBLOCKS for off in offsets]
        shift_bits = [[((shift >> t) & 1) == 1 for t in range(7)] for shift in shifts]

        def turned(tile, x):
            for t in range(7):
                tile = jnp.where(shift_bits[x][t], pltpu.roll(tile, 1 << t, 1), tile)
            return tile


        cols_last = gathered(2)

        def late(a, carry):
            rows = pl.ds(pl.multiple_of(a * KWIDE, 32), KWIDE)
            real, imag = partial(rows, cols_last)
            real, imag = real + acc[rows, : 2 * LANES], imag + acc[rows, 2 * LANES :]
            p, q = real[:, :LANES], real[:, LANES:]
            r, s = imag[:, :LANES], imag[:, LANES:]
            for x, value in enumerate((p - r, q + s, q - s, p + r)):
                part = slice(x * LANES, (x + 1) * LANES)
                sq_hi[rows, part], sq_lo[rows, part] = halves(value * value)
            return carry

        lax.fori_loop(0, KSPAN // KWIDE, late, 0)
        energy = lax.dot_general(gather, sq_hi[...], NT_DIMS, preferred_element_type=jnp.float32)
        energy = energy + lax.dot_general(gather, sq_lo[...], NT_DIMS, preferred_element_type=jnp.float32)
        tiles = [energy[:, a * LANES : (a + 1) * LANES] for a in range(KBLOCKS)]
        for x in (0, 2):
            for a in range(KBLOCKS):
                tile = tiles[a][16 * x : 16 * x + 16]
                cand[x, a] = turned(tile, x) if x else tile
        ahead = jnp.concatenate([tile[16 * x : 16 * x + 16] for x in (1, 3) for tile in reversed(tiles)], axis=0)
        e_hi, e_lo = halves(ahead)
        back = dot(e_hi, flip) + dot(e_lo, flip)
        for x in (1, 3):
            for a in range(KBLOCKS):
                at = (x // 2 * KBLOCKS + a) * 16
                cand[x, a] = turned(back[at : at + 16], x)

        lane = lax.broadcasted_iota(jnp.int32, (16, LANES), 1)

        for t in range(TILES):
            place = t * LANES + lane
            picked = []
            for x in range(4):
                here = jnp.clip(t - heads[x], 0, KBLOCKS - 1)
                before = jnp.clip(t - heads[x] - 1, 0, KBLOCKS - 1)
                picked.append(jnp.where(lane >= shifts[x], cand[x, here], cand[x, before]))
            value = jnp.where(place < count, picked[3], -1.0)
            value = jnp.where(place <= 3 * quarter, picked[2], value)
            value = jnp.where(place <= 2 * quarter, picked[1], value)
            value = jnp.where(place <= quarter, picked[0], value)
            energy_out[pl.ds(t, 16, stride=ROWTILES), :] = value
        for t in range(TILES, ROWTILES):
            energy_out[pl.ds(t, 16, stride=ROWTILES), :] = jnp.zeros((16, LANES), jnp.float32)

        half, band = wave // 8, lax.rem(wave, 8)
        member = half * LEVS + lev

        def rows_of(k):
            return pl.ds(pl.multiple_of(k * ROWTILES, 8), ROWTILES)

        def send_back(d, carry):
            k = member ^ d
            pltpu.make_async_remote_copy(
                src_ref=energy_out.at[rows_of(k)],
                dst_ref=got.at[rows_of(member)],
                send_sem=back_send,
                recv_sem=back_recv,
                device_id=(band + 8 * (k >> 3), k & 7),
                device_id_type=MESH,
            ).start()
            return carry

        lax.fori_loop(1, 16, send_back, 0)
        mine = pltpu.make_async_copy(energy_out.at[rows_of(member)], got.at[rows_of(member)], own_sem.at[0])
        mine.start()
        mine.wait()

        @pl.when(odd)
        def _():
            for t in range(STEPS):
                near_copy(t).wait_send()

        for part in range(3):
            left(part)
        part = pl.ds(0, 15 * ROWTILES)
        pltpu.make_async_copy(energy_out.at[part], energy_out.at[part], back_send).wait()
        pltpu.make_async_copy(got.at[part], got.at[part], back_recv).wait()

        for t in range(TILES):
            out_ref[0, :, t * LANES : (t + 1) * LANES] = got[pl.ds(t, 16, stride=ROWTILES), :]


def local(spectral, legendre, wave_map, row_points, brackets, lev_weight, climatology):
    smem = pl.BlockSpec(memory_space=pltpu.SMEM)
    vmem = pl.BlockSpec(memory_space=pltpu.VMEM)
    hbm = pl.BlockSpec(memory_space=pl.ANY)
    rows = SLOTS * PER_SLOT
    f32, bf16, dma = jnp.float32, jnp.bfloat16, pltpu.SemaphoreType.DMA
    energy = pl.pallas_call(
        kernel,
        grid=(STEPS,),
        out_shape=jax.ShapeDtypeStruct((1, 16, ROWPAD), f32),
        in_specs=[
            smem,
            smem,
            smem,
            smem,
            vmem,
            hbm,
            hbm,
        ],
        out_specs=vmem,
        scratch_shapes=[
            pltpu.VMEM((BUFFERS, STEP_SLOTS, LEV_DEV * COLS, NT), bf16),
            pltpu.VMEM((BUFFERS, STEP_SLOTS, HALF, NT), bf16),
            dma((2, BUFFERS)),
            pltpu.VMEM((rows, HALF), f32),
            pltpu.VMEM((rows, HALF), f32),
            pltpu.VMEM((rows, HALF), f32),
            pltpu.VMEM((HALF * PACK, LANES), f32),
            pltpu.VMEM((DEVICES * PACK, LANES), f32),
            pltpu.VMEM((2, M, LANES), f32),
            pltpu.VMEM((M, LANES), bf16),
            pltpu.VMEM((M, 2 * LANES), bf16),
            pltpu.VMEM((M, 2 * LANES), bf16),
            pltpu.VMEM((M, 2 * LANES), bf16),
            pltpu.VMEM((M, 2 * LANES), bf16),
            pltpu.VMEM((KBLOCK, M), f32),
            pltpu.VMEM((KBLOCK, M), f32),
            pltpu.VMEM((16, M), f32),
            pltpu.VMEM((16, M), f32),
            pltpu.VMEM((KSPAN, M), bf16),
            pltpu.VMEM((KSPAN, M), bf16),
            pltpu.VMEM((KSPAN, M), bf16),
            pltpu.VMEM((KSPAN, M), bf16),
            pltpu.VMEM((KSPAN, 4 * LANES), f32),
            pltpu.VMEM((KSPAN, 4 * LANES), bf16),
            pltpu.VMEM((KSPAN, 4 * LANES), bf16),
            pltpu.VMEM((4, KBLOCKS, 16, LANES), f32),
            pltpu.VMEM((16 * ROWTILES, LANES), f32),
            pltpu.VMEM((16 * ROWTILES, LANES), f32),
            dma((STEPS,)),
            dma((STEPS,)),
            dma((3,)),
            dma((3,)),
            dma((3,)),
            dma,
            dma,
            pltpu.SemaphoreType.REGULAR,
        ],
        compiler_params=pltpu.CompilerParams(
            collective_id=0, has_side_effects=True, vmem_limit_bytes=58 * 1024 * 1024
        ),
        name="transform",
    )(wave_map, brackets, lev_weight, row_points, wave_map, spectral, legendre)
    return jnp.where(energy < 0.0, 0.0, energy - climatology)


def solution(mesh):
    placed = (
        P("wave", "lev", None),
        P("wave", None, None),
        P(),
        P(),
        P(),
        P(),
        P("lev", "wave", None),
    )
    return jax.shard_map(
        local, mesh=mesh, in_specs=placed, out_specs=P("lev", "wave", None), check_vma=False
    )
```

```python
import functools
import math

import jax
import jax.numpy as jnp
from jax import lax
from jax.experimental import pallas as pl
from jax.experimental.pallas import tpu as pltpu
from jax.sharding import PartitionSpec as P

MESH = pl.DeviceIdType.MESH

M = 1280
NT = 1280
LEV_DEV = 4
COLS = 16
HALF = 128
ROWPAD = 5248
LANES = 128

WAVES = 16
LEVS = 8
DEVICES = WAVES * LEVS
SLOTS = M // WAVES
STEP_SLOTS = 8
STEPS = SLOTS // STEP_SLOTS
STEP_ROWS = STEP_SLOTS * 2 * COLS
PER_SLOT = 2 * COLS
GROUPS = SLOTS // 4
PARTS = ((0, 32, 8), (32, 32, 8), (64, 16, 4))
PACK = 2 * GROUPS
PART_AT = (0, 16, 32)
PART_SLOT = (0, WAVES * 32, WAVES * 64)
BUFFERS = 4
STRIDE = 37

KBLOCK = 128
KBLOCKS = 11
KSPAN = KBLOCK * KBLOCKS
KWIDE = 432
KUSED = 3 * KWIDE
TILES = ROWPAD // LANES
ROWTILES = 48

NT_DIMS = (((1,), (1,)), ((), ()))


def pair_of(wave, lev):
    return (wave % 8) * 16 + (wave // 8) * 8 + lev


def turn(product, points):
    inverse = 1.0 / points
    rest = product - jnp.floor(product * inverse + 0.5) * points
    x = rest * (math.pi * inverse)
    y = x * x
    sine = x * (
        1.0
        + y * (-1.0 / 6 + y * (1.0 / 120 + y * (-1.0 / 5040 + y * (1.0 / 362880 - y * (1.0 / 39916800)))))
    )
    cosine = 1.0 + y * (
        -0.5
        + y * (1.0 / 24 + y * (-1.0 / 720 + y * (1.0 / 40320 + y * (-1.0 / 3628800 + y * (1.0 / 479001600)))))
    )
    return 1.0 - 2.0 * (sine * sine), 2.0 * (sine * cosine)


def halves(x):
    high = x.astype(jnp.bfloat16)
    return high, (x - high.astype(jnp.float32)).astype(jnp.bfloat16)


def dot(a, b):
    return jnp.dot(a, b, preferred_element_type=jnp.float32)


def kernel(
    waves_hbm, brackets_hbm, weight_hbm, points_hbm, spec_hbm, leg_hbm, out_ref,
    waves_ref, brackets_ref, weight_ref, points_ref, orders_ref, small_sem, spec_ref, leg_ref, load_sem, mixed, first, other, send, recv, coef, sign, re_hi, re_lo, im_hi, im_lo,
    fine_c, fine_s, coarse_c, coarse_s, cos_hi, cos_lo, sin_hi, sin_lo, acc, sq_hi, sq_lo, cand, energy_out, got,
    near_send, near_recv, far_send, far_recv, own_sem, back_send, back_recv, ready,
):
    step = pl.program_id(0)
    wave, lev = lax.axis_index("wave"), lax.axis_index("lev")
    me = wave * LEVS + lev
    barrier = pltpu.get_barrier_semaphore()

    def loads(t):
        slot = lax.rem(t, BUFFERS)
        at = pl.ds(pl.multiple_of(t * STEP_SLOTS, STEP_SLOTS), STEP_SLOTS)
        return (
            pltpu.make_async_copy(spec_hbm.at[at], spec_ref.at[slot], load_sem.at[0, slot]),
            pltpu.make_async_copy(leg_hbm.at[at], leg_ref.at[slot], load_sem.at[1, slot]),
        )

    smalls = [
        pltpu.make_async_copy(source, target, small_sem.at[i])
        for i, (source, target) in enumerate(
            (
                (brackets_hbm, brackets_ref),
                (weight_hbm, weight_ref),
                (waves_hbm, waves_ref),
                (points_hbm, points_ref),
                (waves_hbm, orders_ref),
            )
        )
    ]

    @pl.when(step == 0)
    def _():
        for small in smalls:
            small.start()
        for t in range(BUFFERS - 1):
            for load in loads(t):
                load.start()

    @pl.when(step + BUFFERS - 1 < STEPS)
    def _():
        for load in loads(step + BUFFERS - 1):
            load.start()

    @pl.when(step == 0)
    def _():
        for d in range(1, LEVS):
            pl.semaphore_signal(
                barrier, inc=1, device_id=(wave, lax.rem(lev + d, LEVS)), device_id_type=MESH
            )
        for d in range(1, WAVES):
            pl.semaphore_signal(
                barrier, inc=1, device_id=(lax.rem(wave + d, WAVES), lev), device_id_type=MESH
            )

    @pl.when(step == 0)
    def _():
        for small in smalls:
            small.wait()

    lower = brackets_ref[lev] - lev * LEV_DEV
    weight = weight_ref[lev]
    gain = jnp.where(lower == LEV_DEV - 1, 1.0 - weight, 0.0)
    odd = (lev & 1) == 1
    even = (lev & 1) == 0
    wide = even & (lev > 0)
    narrow = odd | (lev == 0)
    prior = jnp.maximum(lev - 1, 0)
    prior_last = (brackets_ref[prior] == prior * LEV_DEV + LEV_DEV - 1) & (lev > 0)
    prior_gain = jnp.where(prior_last, 1.0 - weight_ref[prior], 0.0)
    level_weight = [
        jnp.where(lower == v, weight, 0.0) + jnp.where(lower + 1 == v, 1.0 - weight, 0.0) for v in range(LEV_DEV)
    ]

    def near_copy(t):
        rows = pl.ds(pl.multiple_of(t * STEP_ROWS, STEP_ROWS), STEP_ROWS)
        return pltpu.make_async_remote_copy(
            src_ref=first.at[rows],
            dst_ref=other.at[rows],
            send_sem=near_send.at[t],
            recv_sem=near_recv.at[t],
            device_id=(wave, lev ^ 1),
            device_id_type=MESH,
        )

    def assemble(g, slot_of, turn_by, value, row):
        pieces = []
        for c in range(8):
            b = (c - turn_by + 8) & 7
            base = slot_of(b >> 1) * PER_SLOT + (b & 1)
            for hemi in range(2):
                pieces.append(value(pl.ds(base + hemi * COLS, 8, stride=2)))
        send[pl.ds(row, HALF, stride=PACK), :] = jnp.concatenate(pieces, axis=0).T

    def assemble_part(part):
        begin, slots, count = PARTS[part]
        at = PART_AT[part]

        @pl.when(even)
        def _():
            for t in range(begin // STEP_SLOTS, (begin + slots) // STEP_SLOTS):
                near_copy(t).wait_recv()

            def one(r, carry):
                slot_of = lambda u: begin + count * u + r
                assemble(r, slot_of, lev, lambda rows: mixed[rows, :] + gain * other[rows, :], at + r)
                assemble(r, slot_of, lev - 1, lambda rows: prior_gain * first[rows, :], at + count + r)
                return carry

            lax.fori_loop(0, count, one, 0)

        @pl.when(odd)
        def _():
            def one(r, carry):
                assemble(r, lambda u: begin + count * u + r, lev, lambda rows: mixed[rows, :], at + r)
                return carry

            lax.fori_loop(0, count, one, 0)

    def push(part):
        at, count = PART_AT[part], PARTS[part][2]

        def send_rows(height):
            def one(i, carry):
                d = (STRIDE * i) & (DEVICES - 1)
                dw, dl = d >> 3, d & 7
                pair = pair_of(wave, lev) ^ (((dw & 7) << 4) | ((dw >> 3) << 3) | dl)
                pltpu.make_async_remote_copy(
                    src_ref=send.at[pl.ds(pl.multiple_of(pair * PACK + at, 8), height)],
                    dst_ref=recv.at[pl.ds(pl.multiple_of(me * PACK + at, 8), height)],
                    send_sem=far_send.at[part],
                    recv_sem=far_recv.at[part],
                    device_id=(wave ^ dw, lev ^ dl),
                    device_id_type=MESH,
                ).start()
                return carry

            lax.fori_loop(1, DEVICES, one, 0)

        if count == 8:
            pl.when(wide)(lambda: send_rows(16))
            pl.when(narrow)(lambda: send_rows(8))
        else:
            send_rows(8)
        mine = pl.multiple_of(pair_of(wave, lev) * PACK + at, 8)
        pltpu.make_async_copy(
            send.at[pl.ds(mine, 2 * count)],
            recv.at[pl.ds(pl.multiple_of(me * PACK + at, 8), 2 * count)],
            own_sem.at[part],
        ).start()

    def all_of(part, sem, wide_rows, narrow_rows):
        def wait(rows):
            block = recv.at[pl.ds(0, rows)]
            pltpu.make_async_copy(block, block, sem.at[part]).wait()

        if PARTS[part][2] == 8:
            pl.when(wide)(lambda: wait(wide_rows))
            pl.when(narrow)(lambda: wait(narrow_rows))
        else:
            wait((DEVICES - 1) * 8)

    def arrive(part):
        mine = recv.at[pl.ds(0, 2 * PARTS[part][2])]
        pltpu.make_async_copy(mine, mine, own_sem.at[part]).wait()
        wides = WAVES * (LEVS // 2 - 1)
        total = wides * 16 + (DEVICES - wides) * 8
        all_of(part, far_recv, total - 16, total - 8)

    def left(part):
        all_of(part, far_send, (DEVICES - 1) * 16, (DEVICES - 1) * 8)

    @pl.when(step == 2)
    def _():
        pl.semaphore_wait(barrier, LEVS + WAVES - 2)
        for d in range(1, LEVS):
            pl.semaphore_signal(
                ready, inc=1, device_id=(wave, lax.rem(lev + d, LEVS)), device_id_type=MESH
            )

        @pl.when(odd)
        def _():
            near_copy(0).start()
            near_copy(1).start()

    @pl.when(step == 0)
    def _():
        for part in range(3):
            _, _, count = PARTS[part]
            for r in range(count):
                send[pl.ds(PART_AT[part] + count + r, HALF, stride=PACK), :] = jnp.zeros((HALF, LANES), jnp.float32)

    @pl.when(step == 4)
    def _():
        assemble_part(0)
        pl.semaphore_wait(ready, LEVS - 1)
        push(0)

    @pl.when(step == STEPS - 1)
    def _():
        assemble_part(1)
        push(1)

    for load in loads(step):
        load.wait()
    held_at = lax.rem(step, BUFFERS)
    degree = lax.broadcasted_iota(jnp.int32, (1, NT), 1)
    for i in range(STEP_SLOTS):
        order = waves_ref[wave * SLOTS + step * STEP_SLOTS + i]
        kept = jnp.where(degree >= order, 1.0, 0.0)
        signed = kept * (1 - 2 * ((degree + order) & 1)).astype(jnp.float32)
        kept, signed = kept.astype(jnp.bfloat16), signed.astype(jnp.bfloat16)
        coeffs = spec_ref[held_at, i]
        both = jnp.concatenate([coeffs * kept, coeffs * signed], axis=0)
        sums = lax.dot_general(both, leg_ref[held_at, i], NT_DIMS, preferred_element_type=jnp.float32)
        base = step * STEP_ROWS + i * PER_SLOT
        for hemi in range(2):
            own = [sums[(LEV_DEV * hemi + v) * COLS : (LEV_DEV * hemi + v + 1) * COLS] for v in range(LEV_DEV)]
            at = pl.ds(pl.multiple_of(base + hemi * COLS, COLS), COLS)
            total = own[0] * level_weight[0]
            for v in range(1, LEV_DEV):
                total = total + own[v] * level_weight[v]
            mixed[at, :] = total
            first[at, :] = own[0]

    @pl.when(odd & (step > 1))
    def _():
        near_copy(step).start()

    @pl.when(step == STEPS - 1)
    def _():
        assemble_part(2)
        push(2)

        count = points_ref[pair_of(wave, lev)]
        points = count.astype(jnp.float32)
        natural = orders_ref[...].reshape(1, M).astype(jnp.float32)
        pieces = []
        for begin, slots, _ in PARTS:
            pieces += [natural[:, w * SLOTS + begin : w * SLOTS + begin + slots] for w in range(WAVES)]
        orders = jnp.concatenate(pieces, axis=1)
        fine_k = lax.broadcasted_iota(jnp.int32, (KBLOCK, 1), 0).astype(jnp.float32)
        fine_c[...], fine_s[...] = turn(fine_k * orders, points)
        coarse_k = lax.broadcasted_iota(jnp.int32, (16, 1), 0).astype(jnp.float32) * KBLOCK
        factor = jnp.where(orders == 0.0, 1.0, 2.0)
        factor = jnp.where(orders <= ((count - 1) // 2).astype(jnp.float32), factor, 0.0)
        whole_c, whole_s = turn(coarse_k * orders, points)
        coarse_c[...] = whole_c * factor
        coarse_s[...] = whole_s * factor

        def basis(a, carry):
            cc, cs = coarse_c[pl.ds(a, 1), :], coarse_s[pl.ds(a, 1), :]
            at = pl.ds(pl.multiple_of(a * KBLOCK, KBLOCK), KBLOCK)
            for lanes in range(0, M, 256):
                part = slice(lanes, lanes + 256)
                fc, fs = fine_c[:, part], fine_s[:, part]
                c, s = cc[:, part], cs[:, part]
                cos_hi[at, part], cos_lo[at, part] = halves(fc * c - fs * s)
                sin_hi[at, part], sin_lo[at, part] = halves(fs * c + fc * s)
            return carry

        lax.fori_loop(0, KBLOCKS, basis, 0)
        parity = (1 - 2 * (orders.astype(jnp.int32) & 1)).astype(jnp.float32)
        for i in range(0, M, LANES):
            wide = jnp.broadcast_to(parity[:, i : i + LANES], (LANES, LANES))
            sign[i : i + LANES, :] = wide.T.astype(jnp.bfloat16)

        lane_block = lax.broadcasted_iota(jnp.int32, (8, LANES), 1) // COLS
        bits = [((lane_block >> t) & 1) == 1 for t in range(3)]

        def spread(w, part):
            _, slots, count = PARTS[part]
            at = [(w * LEVS + p) * PACK + PART_AT[part] for p in range(LEVS)]
            held = [recv[at[p] : at[p] + 8, :] for p in range(LEVS)]
            for p in range(1, LEVS - 1, 2):
                if count == 8:
                    held[p] = held[p] + recv[at[p + 1] + 8 : at[p + 1] + 16, :]
                else:
                    held[p] = held[p] + pltpu.roll(held[p + 1], 4, 0)
            for t in range(3):
                held = [jnp.where(bits[t], held[(x + (1 << t)) % 8], held[x]) for x in range(8)]
            for b in range(8):
                moved = held[-b % 8]
                if b:
                    moved = pltpu.roll(moved, LANES - COLS * b, 1)
                base = PART_SLOT[part] + w * slots + count * (b // 2)
                coef[b % 2, base : base + count, :] = moved[:count]

        def split(low, high):
            at = slice(low, high)
            flip_sign = sign[at, :]
            for part, (high_ref, low_ref) in enumerate(((re_hi, re_lo), (im_hi, im_lo))):
                for ref, value in zip((high_ref, low_ref), halves(coef[part, at, :])):
                    ref[at, :LANES] = value
                    ref[at, LANES:] = value * flip_sign

        def partial(rows, cols):
            real = dot(cos_hi[rows, cols], re_hi[cols, :]) + dot(cos_lo[rows, cols], re_hi[cols, :])
            real = real + dot(cos_hi[rows, cols], re_lo[cols, :])
            imag = dot(sin_hi[rows, cols], im_hi[cols, :]) + dot(sin_lo[rows, cols], im_hi[cols, :])
            imag = imag + dot(sin_hi[rows, cols], im_lo[cols, :])
            return real, imag

        def gathered(part):
            arrive(part)
            for w in range(WAVES):
                spread(w, part)
            begin = PART_SLOT[part]
            split(begin, begin + WAVES * PARTS[part][1])
            return slice(begin, begin + WAVES * PARTS[part][1])

        cols = gathered(0)

        def early(a, carry):
            rows = pl.ds(pl.multiple_of(a * KWIDE, 16), KWIDE)
            acc[rows, : 2 * LANES], acc[rows, 2 * LANES :] = partial(rows, cols)
            return carry

        lax.fori_loop(0, KUSED // KWIDE, early, 0)
        cols_next = gathered(1)

        def second(a, carry):
            rows = pl.ds(pl.multiple_of(a * KWIDE, 16), KWIDE)
            real, imag = partial(rows, cols_next)
            acc[rows, : 2 * LANES] = acc[rows, : 2 * LANES] + real
            acc[rows, 2 * LANES :] = acc[rows, 2 * LANES :] + imag
            return carry

        lax.fori_loop(0, KUSED // KWIDE, second, 0)

        row = lax.broadcasted_iota(jnp.int32, (64, 4 * LANES), 0)
        col = lax.broadcasted_iota(jnp.int32, (64, 4 * LANES), 1)
        belongs = (
            ((row >> 4) == (col >> 7)) & ((row & 7) == ((col >> 4) & 7)) & (((row >> 3) & 1) == ((col >> 3) & 1))
        )
        gather = jnp.where(belongs, 0.125, 0.0).astype(jnp.bfloat16)
        quarter = count // 4
        offsets = (0, 2 * quarter - (KSPAN - 1), 2 * quarter, 4 * quarter - (KSPAN - 1))
        shifts = [lax.rem(off + KSPAN, LANES) for off in offsets]
        heads = [(off + KSPAN) // LANES - KBLOCKS for off in offsets]
        old = lax.broadcasted_iota(jnp.int32, (LANES, LANES), 0)
        new = lax.broadcasted_iota(jnp.int32, (LANES, LANES), 1)
        places = [None] + [
            jnp.where((((LANES - 1 - old) if x % 2 else old) + shifts[x]) & (LANES - 1) == new, 1.0, 0.0)
            for x in (1, 2, 3)
        ]
        sq_hi[KUSED:, :] = jnp.zeros((KSPAN - KUSED, 4 * LANES), jnp.bfloat16)
        sq_lo[KUSED:, :] = jnp.zeros((KSPAN - KUSED, 4 * LANES), jnp.bfloat16)

        cols_last = gathered(2)

        def late(a, carry):
            rows = pl.ds(pl.multiple_of(a * KWIDE, 16), KWIDE)
            real, imag = partial(rows, cols_last)
            real, imag = real + acc[rows, : 2 * LANES], imag + acc[rows, 2 * LANES :]
            p, q = real[:, :LANES], real[:, LANES:]
            r, s = imag[:, :LANES], imag[:, LANES:]
            for x, value in enumerate((p - r, q + s, q - s, p + r)):
                part = slice(x * LANES, (x + 1) * LANES)
                sq_hi[rows, part], sq_lo[rows, part] = halves(value * value)
            return carry

        lax.fori_loop(0, KUSED // KWIDE, late, 0)
        energy = lax.dot_general(gather, sq_hi[...], NT_DIMS, preferred_element_type=jnp.float32)
        energy = energy + lax.dot_general(gather, sq_lo[...], NT_DIMS, preferred_element_type=jnp.float32)
        tiles = [energy[:, a * LANES : (a + 1) * LANES] for a in range(KBLOCKS)]
        for x in range(4):
            own = [tile[16 * x : 16 * x + 16] for tile in (reversed(tiles) if x % 2 else tiles)]
            if x:
                high, low = halves(jnp.concatenate(own, axis=0))
                place = places[x].astype(jnp.bfloat16)
                moved = dot(high, place) + dot(low, place)
                own = [moved[16 * a : 16 * a + 16] for a in range(KBLOCKS)]
            for a in range(KBLOCKS):
                cand[x, a] = own[a]

        lane = lax.broadcasted_iota(jnp.int32, (16, LANES), 1)

        def tile_at(t):
            place = t * LANES + lane
            picked = []
            for x in range(4):
                here = jnp.clip(t - heads[x], 0, KBLOCKS - 1)
                before = jnp.clip(t - heads[x] - 1, 0, KBLOCKS - 1)
                picked.append(jnp.where(lane >= shifts[x], cand[x, here], cand[x, before]))
            value = jnp.where(place < count, picked[3], -1.0)
            value = jnp.where(place <= 3 * quarter, picked[2], value)
            value = jnp.where(place <= 2 * quarter, picked[1], value)
            value = jnp.where(place <= quarter, picked[0], value)
            energy_out[pl.ds(t, 16, stride=ROWTILES), :] = value

        half, band = wave // 8, lax.rem(wave, 8)
        member = half * LEVS + lev

        def rows_of(k, piece):
            return pl.ds(pl.multiple_of(k * ROWTILES + piece * 16, 8), 16)

        for piece in range(3):
            for t in range(piece * 16, piece * 16 + 16):
                if t < TILES:
                    tile_at(t)
                else:
                    energy_out[pl.ds(t, 16, stride=ROWTILES), :] = jnp.zeros((16, LANES), jnp.float32)

            def send_back(d, carry):
                k = member ^ (16 - d)
                pltpu.make_async_remote_copy(
                    src_ref=energy_out.at[rows_of(k, piece)],
                    dst_ref=got.at[rows_of(member, piece)],
                    send_sem=back_send,
                    recv_sem=back_recv,
                    device_id=(band + 8 * (k >> 3), k & 7),
                    device_id_type=MESH,
                ).start()
                return carry

            lax.fori_loop(1, 16, send_back, 0)
        whole = pl.ds(pl.multiple_of(member * ROWTILES, 8), ROWTILES)
        mine = pltpu.make_async_copy(energy_out.at[whole], got.at[whole], own_sem.at[0])
        mine.start()
        mine.wait()

        @pl.when(odd)
        def _():
            for t in range(STEPS):
                near_copy(t).wait_send()

        for part in range(3):
            left(part)
        part = pl.ds(0, 15 * ROWTILES)
        pltpu.make_async_copy(energy_out.at[part], energy_out.at[part], back_send).wait()
        pltpu.make_async_copy(got.at[part], got.at[part], back_recv).wait()

        for t in range(TILES):
            out_ref[0, :, t * LANES : (t + 1) * LANES] = got[pl.ds(t, 16, stride=ROWTILES), :]


def local(spectral, legendre, wave_map, row_points, brackets, lev_weight, climatology):
    vmem = pl.BlockSpec(memory_space=pltpu.VMEM)
    hbm = pl.BlockSpec(memory_space=pltpu.HBM)
    rows = SLOTS * PER_SLOT
    f32, bf16, dma = jnp.float32, jnp.bfloat16, pltpu.SemaphoreType.DMA
    energy = pl.pallas_call(
        kernel,
        grid=(STEPS,),
        out_shape=jax.ShapeDtypeStruct((1, 16, ROWPAD), f32),
        in_specs=[
            hbm,
            hbm,
            hbm,
            hbm,
            hbm,
            hbm,
        ],
        out_specs=vmem,
        scratch_shapes=[
            pltpu.SMEM((M,), jnp.int32),
            pltpu.SMEM((LEVS,), jnp.int32),
            pltpu.SMEM((LEVS,), f32),
            pltpu.SMEM((HALF,), jnp.int32),
            pltpu.VMEM((M,), jnp.int32),
            dma((5,)),
            pltpu.VMEM((BUFFERS, STEP_SLOTS, LEV_DEV * COLS, NT), bf16),
            pltpu.VMEM((BUFFERS, STEP_SLOTS, HALF, NT), bf16),
            dma((2, BUFFERS)),
            pltpu.VMEM((rows, HALF), f32),
            pltpu.VMEM((rows, HALF), f32),
            pltpu.VMEM((rows, HALF), f32),
            pltpu.VMEM((HALF * PACK, LANES), f32),
            pltpu.VMEM((DEVICES * PACK, LANES), f32),
            pltpu.VMEM((2, M, LANES), f32),
            pltpu.VMEM((M, LANES), bf16),
            pltpu.VMEM((M, 2 * LANES), bf16),
            pltpu.VMEM((M, 2 * LANES), bf16),
            pltpu.VMEM((M, 2 * LANES), bf16),
            pltpu.VMEM((M, 2 * LANES), bf16),
            pltpu.VMEM((KBLOCK, M), f32),
            pltpu.VMEM((KBLOCK, M), f32),
            pltpu.VMEM((16, M), f32),
            pltpu.VMEM((16, M), f32),
            pltpu.VMEM((KSPAN, M), bf16),
            pltpu.VMEM((KSPAN, M), bf16),
            pltpu.VMEM((KSPAN, M), bf16),
            pltpu.VMEM((KSPAN, M), bf16),
            pltpu.VMEM((KSPAN, 4 * LANES), f32),
            pltpu.VMEM((KSPAN, 4 * LANES), bf16),
            pltpu.VMEM((KSPAN, 4 * LANES), bf16),
            pltpu.VMEM((4, KBLOCKS, 16, LANES), f32),
            pltpu.VMEM((16 * ROWTILES, LANES), f32),
            pltpu.VMEM((16 * ROWTILES, LANES), f32),
            dma((STEPS,)),
            dma((STEPS,)),
            dma((3,)),
            dma((3,)),
            dma((3,)),
            dma,
            dma,
            pltpu.SemaphoreType.REGULAR,
        ],
        compiler_params=pltpu.CompilerParams(
            collective_id=0, has_side_effects=True, vmem_limit_bytes=58 * 1024 * 1024
        ),
        name="transform",
    )(wave_map, brackets, lev_weight, row_points, spectral, legendre)
    return jnp.where(energy < 0.0, 0.0, energy - climatology)


def solution(mesh):
    placed = (
        P("wave", "lev", None),
        P("wave", None, None),
        P(),
        P(),
        P(),
        P(),
        P("lev", "wave", None),
    )
    return jax.shard_map(
        local, mesh=mesh, in_specs=placed, out_specs=P("lev", "wave", None), check_vma=False
    )
```

```python
import functools
import math

import jax
import jax.numpy as jnp
from jax import lax
from jax.experimental import pallas as pl
from jax.experimental.pallas import tpu as pltpu
from jax.sharding import PartitionSpec as P

MESH = pl.DeviceIdType.MESH

M = 1280
NT = 1280
LEV_DEV = 4
COLS = 16
HALF = 128
ROWPAD = 5248
LANES = 128

WAVES = 16
LEVS = 8
DEVICES = WAVES * LEVS
SLOTS = M // WAVES
STEP_SLOTS = 8
STEPS = SLOTS // STEP_SLOTS
STEP_ROWS = STEP_SLOTS * 2 * COLS
PER_SLOT = 2 * COLS
GROUPS = SLOTS // 4
PARTS = ((0, 32, 8), (32, 32, 8), (64, 16, 4))
PACK = 2 * GROUPS
PART_AT = (0, 16, 32)
PART_SLOT = (0, WAVES * 32, WAVES * 64)
BUFFERS = 4
SCALE = float(2**28)
AT_POINTS = M
AT_BRACKETS = M + HALF
AT_WEIGHT = AT_BRACKETS + LEVS
SMALL = AT_WEIGHT + LEVS
STRIDE = 37

KBLOCK = 128
KBLOCKS = 11
KSPAN = KBLOCK * KBLOCKS
KWIDE = 432
KUSED = 3 * KWIDE
TILES = ROWPAD // LANES
ROWTILES = 48

NT_DIMS = (((1,), (1,)), ((), ()))


def pair_of(wave, lev):
    return (wave % 8) * 16 + (wave // 8) * 8 + lev


def turn(product, points):
    inverse = 1.0 / points
    rest = product - jnp.floor(product * inverse + 0.5) * points
    x = rest * (math.pi * inverse)
    y = x * x
    sine = x * (
        1.0
        + y * (-1.0 / 6 + y * (1.0 / 120 + y * (-1.0 / 5040 + y * (1.0 / 362880 - y * (1.0 / 39916800)))))
    )
    cosine = 1.0 + y * (
        -0.5
        + y * (1.0 / 24 + y * (-1.0 / 720 + y * (1.0 / 40320 + y * (-1.0 / 3628800 + y * (1.0 / 479001600)))))
    )
    return 1.0 - 2.0 * (sine * sine), 2.0 * (sine * cosine)


def halves(x):
    high = x.astype(jnp.bfloat16)
    return high, (x - high.astype(jnp.float32)).astype(jnp.bfloat16)


def dot(a, b):
    return jnp.dot(a, b, preferred_element_type=jnp.float32)


def kernel(
    small_hbm, spec_hbm, leg_hbm, out_ref,
    small_ref, orders_ref, small_sem, spec_ref, leg_ref, load_sem, mixed, first, other, send, recv, coef, sign, re_hi, re_lo, im_hi, im_lo,
    fine_c, fine_s, coarse_c, coarse_s, cos_hi, cos_lo, sin_hi, sin_lo, acc, sq_hi, sq_lo, cand, energy_out, got,
    near_send, near_recv, far_send, far_recv, own_sem, back_send, back_recv, ready,
):
    step = pl.program_id(0)
    wave, lev = lax.axis_index("wave"), lax.axis_index("lev")
    me = wave * LEVS + lev
    barrier = pltpu.get_barrier_semaphore()

    def loads(t):
        slot = lax.rem(t, BUFFERS)
        at = pl.ds(pl.multiple_of(t * STEP_SLOTS, STEP_SLOTS), STEP_SLOTS)
        return (
            pltpu.make_async_copy(spec_hbm.at[at], spec_ref.at[slot], load_sem.at[0, slot]),
            pltpu.make_async_copy(leg_hbm.at[at], leg_ref.at[slot], load_sem.at[1, slot]),
        )

    smalls = [
        pltpu.make_async_copy(source, target, small_sem.at[i])
        for i, (source, target) in enumerate(
            (
                (small_hbm, small_ref),
                (small_hbm, orders_ref),
            )
        )
    ]

    @pl.when(step == 0)
    def _():
        for small in smalls:
            small.start()
        for t in range(BUFFERS - 1):
            for load in loads(t):
                load.start()

    @pl.when(step + BUFFERS - 1 < STEPS)
    def _():
        for load in loads(step + BUFFERS - 1):
            load.start()

    @pl.when(step == 0)
    def _():
        for d in range(1, LEVS):
            pl.semaphore_signal(
                barrier, inc=1, device_id=(wave, lax.rem(lev + d, LEVS)), device_id_type=MESH
            )
        for d in range(1, WAVES):
            pl.semaphore_signal(
                barrier, inc=1, device_id=(lax.rem(wave + d, WAVES), lev), device_id_type=MESH
            )

    @pl.when(step == 0)
    def _():
        for small in smalls:
            small.wait()

    lower = small_ref[AT_BRACKETS + lev] - lev * LEV_DEV
    weight = small_ref[AT_WEIGHT + lev].astype(jnp.float32) * (1.0 / SCALE)
    gain = jnp.where(lower == LEV_DEV - 1, 1.0 - weight, 0.0)
    odd = (lev & 1) == 1
    even = (lev & 1) == 0
    wide = even & (lev > 0)
    narrow = odd | (lev == 0)
    prior = jnp.maximum(lev - 1, 0)
    prior_last = (small_ref[AT_BRACKETS + prior] == prior * LEV_DEV + LEV_DEV - 1) & (lev > 0)
    prior_gain = jnp.where(prior_last, 1.0 - small_ref[AT_WEIGHT + prior].astype(jnp.float32) * (1.0 / SCALE), 0.0)
    level_weight = [
        jnp.where(lower == v, weight, 0.0) + jnp.where(lower + 1 == v, 1.0 - weight, 0.0) for v in range(LEV_DEV)
    ]

    def near_copy(t):
        rows = pl.ds(pl.multiple_of(t * STEP_ROWS, STEP_ROWS), STEP_ROWS)
        return pltpu.make_async_remote_copy(
            src_ref=first.at[rows],
            dst_ref=other.at[rows],
            send_sem=near_send.at[t],
            recv_sem=near_recv.at[t],
            device_id=(wave, lev ^ 1),
            device_id_type=MESH,
        )

    def assemble(g, slot_of, turn_by, value, row):
        pieces = []
        for c in range(8):
            b = (c - turn_by + 8) & 7
            base = slot_of(b >> 1) * PER_SLOT + (b & 1)
            for hemi in range(2):
                pieces.append(value(pl.ds(base + hemi * COLS, 8, stride=2)))
        send[pl.ds(row, HALF, stride=PACK), :] = jnp.concatenate(pieces, axis=0).T

    def assemble_part(part):
        begin, slots, count = PARTS[part]
        at = PART_AT[part]

        @pl.when(even)
        def _():
            for t in range(begin // STEP_SLOTS, (begin + slots) // STEP_SLOTS):
                near_copy(t).wait_recv()

            def one(r, carry):
                slot_of = lambda u: begin + count * u + r
                assemble(r, slot_of, lev, lambda rows: mixed[rows, :] + gain * other[rows, :], at + r)
                assemble(r, slot_of, lev - 1, lambda rows: prior_gain * first[rows, :], at + count + r)
                return carry

            lax.fori_loop(0, count, one, 0)

        @pl.when(odd)
        def _():
            def one(r, carry):
                assemble(r, lambda u: begin + count * u + r, lev, lambda rows: mixed[rows, :], at + r)
                return carry

            lax.fori_loop(0, count, one, 0)

    def push(part):
        at, count = PART_AT[part], PARTS[part][2]

        def send_rows(height):
            def one(i, carry):
                d = (STRIDE * i) & (DEVICES - 1)
                dw, dl = d >> 3, d & 7
                pair = pair_of(wave, lev) ^ (((dw & 7) << 4) | ((dw >> 3) << 3) | dl)
                pltpu.make_async_remote_copy(
                    src_ref=send.at[pl.ds(pl.multiple_of(pair * PACK + at, 8), height)],
                    dst_ref=recv.at[pl.ds(pl.multiple_of(me * PACK + at, 8), height)],
                    send_sem=far_send.at[part],
                    recv_sem=far_recv.at[part],
                    device_id=(wave ^ dw, lev ^ dl),
                    device_id_type=MESH,
                ).start()
                return carry

            lax.fori_loop(1, DEVICES, one, 0)

        if count == 8:
            pl.when(wide)(lambda: send_rows(16))
            pl.when(narrow)(lambda: send_rows(8))
        else:
            send_rows(8)
        mine = pl.multiple_of(pair_of(wave, lev) * PACK + at, 8)
        pltpu.make_async_copy(
            send.at[pl.ds(mine, 2 * count)],
            recv.at[pl.ds(pl.multiple_of(me * PACK + at, 8), 2 * count)],
            own_sem.at[part],
        ).start()

    def all_of(part, sem, wide_rows, narrow_rows):
        def wait(rows):
            block = recv.at[pl.ds(0, rows)]
            pltpu.make_async_copy(block, block, sem.at[part]).wait()

        if PARTS[part][2] == 8:
            pl.when(wide)(lambda: wait(wide_rows))
            pl.when(narrow)(lambda: wait(narrow_rows))
        else:
            wait((DEVICES - 1) * 8)

    def arrive(part):
        mine = recv.at[pl.ds(0, 2 * PARTS[part][2])]
        pltpu.make_async_copy(mine, mine, own_sem.at[part]).wait()
        wides = WAVES * (LEVS // 2 - 1)
        total = wides * 16 + (DEVICES - wides) * 8
        all_of(part, far_recv, total - 16, total - 8)

    def left(part):
        all_of(part, far_send, (DEVICES - 1) * 16, (DEVICES - 1) * 8)

    @pl.when(step == 2)
    def _():
        pl.semaphore_wait(barrier, LEVS + WAVES - 2)
        for d in range(1, LEVS):
            pl.semaphore_signal(
                ready, inc=1, device_id=(wave, lax.rem(lev + d, LEVS)), device_id_type=MESH
            )

        @pl.when(odd)
        def _():
            near_copy(0).start()
            near_copy(1).start()

    @pl.when(step == 0)
    def _():
        for part in range(3):
            _, _, count = PARTS[part]
            for r in range(count):
                send[pl.ds(PART_AT[part] + count + r, HALF, stride=PACK), :] = jnp.zeros((HALF, LANES), jnp.float32)

    @pl.when(step == 4)
    def _():
        assemble_part(0)
        pl.semaphore_wait(ready, LEVS - 1)
        push(0)

    @pl.when(step == STEPS - 1)
    def _():
        assemble_part(1)
        push(1)

    for load in loads(step):
        load.wait()
    held_at = lax.rem(step, BUFFERS)
    degree = lax.broadcasted_iota(jnp.int32, (1, NT), 1)
    for i in range(STEP_SLOTS):
        order = small_ref[wave * SLOTS + step * STEP_SLOTS + i]
        kept = jnp.where(degree >= order, 1.0, 0.0)
        signed = kept * (1 - 2 * ((degree + order) & 1)).astype(jnp.float32)
        kept, signed = kept.astype(jnp.bfloat16), signed.astype(jnp.bfloat16)
        coeffs = spec_ref[held_at, i]
        both = jnp.concatenate([coeffs * kept, coeffs * signed], axis=0)
        sums = lax.dot_general(both, leg_ref[held_at, i], NT_DIMS, preferred_element_type=jnp.float32)
        base = step * STEP_ROWS + i * PER_SLOT
        for hemi in range(2):
            own = [sums[(LEV_DEV * hemi + v) * COLS : (LEV_DEV * hemi + v + 1) * COLS] for v in range(LEV_DEV)]
            at = pl.ds(pl.multiple_of(base + hemi * COLS, COLS), COLS)
            total = own[0] * level_weight[0]
            for v in range(1, LEV_DEV):
                total = total + own[v] * level_weight[v]
            mixed[at, :] = total
            first[at, :] = own[0]

    @pl.when(odd & (step > 1))
    def _():
        near_copy(step).start()

    @pl.when(step == STEPS - 1)
    def _():
        assemble_part(2)
        push(2)

        count = small_ref[AT_POINTS + pair_of(wave, lev)]
        points = count.astype(jnp.float32)
        natural = orders_ref[...][:M].reshape(1, M).astype(jnp.float32)
        pieces = []
        for begin, slots, _ in PARTS:
            pieces += [natural[:, w * SLOTS + begin : w * SLOTS + begin + slots] for w in range(WAVES)]
        orders = jnp.concatenate(pieces, axis=1)
        fine_k = lax.broadcasted_iota(jnp.int32, (KBLOCK, 1), 0).astype(jnp.float32)
        fine_c[...], fine_s[...] = turn(fine_k * orders, points)
        coarse_k = lax.broadcasted_iota(jnp.int32, (16, 1), 0).astype(jnp.float32) * KBLOCK
        factor = jnp.where(orders == 0.0, 1.0, 2.0)
        factor = jnp.where(orders <= ((count - 1) // 2).astype(jnp.float32), factor, 0.0)
        whole_c, whole_s = turn(coarse_k * orders, points)
        coarse_c[...] = whole_c * factor
        coarse_s[...] = whole_s * factor

        def basis(a, carry):
            cc, cs = coarse_c[pl.ds(a, 1), :], coarse_s[pl.ds(a, 1), :]
            at = pl.ds(pl.multiple_of(a * KBLOCK, KBLOCK), KBLOCK)
            for lanes in range(0, M, 256):
                part = slice(lanes, lanes + 256)
                fc, fs = fine_c[:, part], fine_s[:, part]
                c, s = cc[:, part], cs[:, part]
                cos_hi[at, part], cos_lo[at, part] = halves(fc * c - fs * s)
                sin_hi[at, part], sin_lo[at, part] = halves(fs * c + fc * s)
            return carry

        lax.fori_loop(0, KBLOCKS, basis, 0)
        parity = (1 - 2 * (orders.astype(jnp.int32) & 1)).astype(jnp.float32)
        for i in range(0, M, LANES):
            wide = jnp.broadcast_to(parity[:, i : i + LANES], (LANES, LANES))
            sign[i : i + LANES, :] = wide.T.astype(jnp.bfloat16)

        lane_block = lax.broadcasted_iota(jnp.int32, (8, LANES), 1) // COLS
        bits = [((lane_block >> t) & 1) == 1 for t in range(3)]

        def spread(w, part):
            _, slots, count = PARTS[part]
            at = [(w * LEVS + p) * PACK + PART_AT[part] for p in range(LEVS)]
            held = [recv[at[p] : at[p] + 8, :] for p in range(LEVS)]
            for p in range(1, LEVS - 1, 2):
                if count == 8:
                    held[p] = held[p] + recv[at[p + 1] + 8 : at[p + 1] + 16, :]
                else:
                    held[p] = held[p] + pltpu.roll(held[p + 1], 4, 0)
            for t in range(3):
                held = [jnp.where(bits[t], held[(x + (1 << t)) % 8], held[x]) for x in range(8)]
            for b in range(8):
                moved = held[-b % 8]
                if b:
                    moved = pltpu.roll(moved, LANES - COLS * b, 1)
                base = PART_SLOT[part] + w * slots + count * (b // 2)
                coef[b % 2, base : base + count, :] = moved[:count]

        def split(low, high):
            at = slice(low, high)
            flip_sign = sign[at, :]
            for part, (high_ref, low_ref) in enumerate(((re_hi, re_lo), (im_hi, im_lo))):
                for ref, value in zip((high_ref, low_ref), halves(coef[part, at, :])):
                    ref[at, :LANES] = value
                    ref[at, LANES:] = value * flip_sign

        def partial(rows, cols):
            real = dot(cos_hi[rows, cols], re_hi[cols, :]) + dot(cos_lo[rows, cols], re_hi[cols, :])
            real = real + dot(cos_hi[rows, cols], re_lo[cols, :])
            imag = dot(sin_hi[rows, cols], im_hi[cols, :]) + dot(sin_lo[rows, cols], im_hi[cols, :])
            imag = imag + dot(sin_hi[rows, cols], im_lo[cols, :])
            return real, imag

        def gathered(part):
            arrive(part)
            for w in range(WAVES):
                spread(w, part)
            begin = PART_SLOT[part]
            split(begin, begin + WAVES * PARTS[part][1])
            return slice(begin, begin + WAVES * PARTS[part][1])

        cols = gathered(0)

        def early(a, carry):
            rows = pl.ds(pl.multiple_of(a * KWIDE, 16), KWIDE)
            acc[rows, : 2 * LANES], acc[rows, 2 * LANES :] = partial(rows, cols)
            return carry

        lax.fori_loop(0, KUSED // KWIDE, early, 0)
        cols_next = gathered(1)

        def second(a, carry):
            rows = pl.ds(pl.multiple_of(a * KWIDE, 16), KWIDE)
            real, imag = partial(rows, cols_next)
            acc[rows, : 2 * LANES] = acc[rows, : 2 * LANES] + real
            acc[rows, 2 * LANES :] = acc[rows, 2 * LANES :] + imag
            return carry

        lax.fori_loop(0, KUSED // KWIDE, second, 0)

        row = lax.broadcasted_iota(jnp.int32, (64, 4 * LANES), 0)
        col = lax.broadcasted_iota(jnp.int32, (64, 4 * LANES), 1)
        belongs = (
            ((row >> 4) == (col >> 7)) & ((row & 7) == ((col >> 4) & 7)) & (((row >> 3) & 1) == ((col >> 3) & 1))
        )
        gather = jnp.where(belongs, 0.125, 0.0).astype(jnp.bfloat16)
        quarter = count // 4
        offsets = (0, 2 * quarter - (KSPAN - 1), 2 * quarter, 4 * quarter - (KSPAN - 1))
        shifts = [lax.rem(off + KSPAN, LANES) for off in offsets]
        heads = [(off + KSPAN) // LANES - KBLOCKS for off in offsets]
        old = lax.broadcasted_iota(jnp.int32, (LANES, LANES), 0)
        new = lax.broadcasted_iota(jnp.int32, (LANES, LANES), 1)
        places = [None] + [
            jnp.where((((LANES - 1 - old) if x % 2 else old) + shifts[x]) & (LANES - 1) == new, 1.0, 0.0)
            for x in (1, 2, 3)
        ]
        sq_hi[KUSED:, :] = jnp.zeros((KSPAN - KUSED, 4 * LANES), jnp.bfloat16)
        sq_lo[KUSED:, :] = jnp.zeros((KSPAN - KUSED, 4 * LANES), jnp.bfloat16)

        cols_last = gathered(2)

        def late(a, carry):
            rows = pl.ds(pl.multiple_of(a * KWIDE, 16), KWIDE)
            real, imag = partial(rows, cols_last)
            real, imag = real + acc[rows, : 2 * LANES], imag + acc[rows, 2 * LANES :]
            p, q = real[:, :LANES], real[:, LANES:]
            r, s = imag[:, :LANES], imag[:, LANES:]
            for x, value in enumerate((p - r, q + s, q - s, p + r)):
                part = slice(x * LANES, (x + 1) * LANES)
                sq_hi[rows, part], sq_lo[rows, part] = halves(value * value)
            return carry

        lax.fori_loop(0, KUSED // KWIDE, late, 0)
        energy = lax.dot_general(gather, sq_hi[...], NT_DIMS, preferred_element_type=jnp.float32)
        energy = energy + lax.dot_general(gather, sq_lo[...], NT_DIMS, preferred_element_type=jnp.float32)
        tiles = [energy[:, a * LANES : (a + 1) * LANES] for a in range(KBLOCKS)]
        for x in range(4):
            own = [tile[16 * x : 16 * x + 16] for tile in (reversed(tiles) if x % 2 else tiles)]
            if x:
                high, low = halves(jnp.concatenate(own, axis=0))
                place = places[x].astype(jnp.bfloat16)
                moved = dot(high, place) + dot(low, place)
                own = [moved[16 * a : 16 * a + 16] for a in range(KBLOCKS)]
            for a in range(KBLOCKS):
                cand[x, a] = own[a]

        lane = lax.broadcasted_iota(jnp.int32, (16, LANES), 1)

        def tile_at(t):
            place = t * LANES + lane
            picked = []
            for x in range(4):
                here = jnp.clip(t - heads[x], 0, KBLOCKS - 1)
                before = jnp.clip(t - heads[x] - 1, 0, KBLOCKS - 1)
                picked.append(jnp.where(lane >= shifts[x], cand[x, here], cand[x, before]))
            value = jnp.where(place < count, picked[3], -1.0)
            value = jnp.where(place <= 3 * quarter, picked[2], value)
            value = jnp.where(place <= 2 * quarter, picked[1], value)
            value = jnp.where(place <= quarter, picked[0], value)
            energy_out[pl.ds(t, 16, stride=ROWTILES), :] = value

        half, band = wave // 8, lax.rem(wave, 8)
        member = half * LEVS + lev

        def rows_of(k, piece):
            return pl.ds(pl.multiple_of(k * ROWTILES + piece * 16, 8), 16)

        for piece in range(3):
            for t in range(piece * 16, piece * 16 + 16):
                if t < TILES:
                    tile_at(t)
                else:
                    energy_out[pl.ds(t, 16, stride=ROWTILES), :] = jnp.zeros((16, LANES), jnp.float32)

            def send_back(d, carry):
                k = member ^ (16 - d)
                pltpu.make_async_remote_copy(
                    src_ref=energy_out.at[rows_of(k, piece)],
                    dst_ref=got.at[rows_of(member, piece)],
                    send_sem=back_send,
                    recv_sem=back_recv,
                    device_id=(band + 8 * (k >> 3), k & 7),
                    device_id_type=MESH,
                ).start()
                return carry

            lax.fori_loop(1, 16, send_back, 0)
        whole = pl.ds(pl.multiple_of(member * ROWTILES, 8), ROWTILES)
        mine = pltpu.make_async_copy(energy_out.at[whole], got.at[whole], own_sem.at[0])
        mine.start()
        mine.wait()

        @pl.when(odd)
        def _():
            for t in range(STEPS):
                near_copy(t).wait_send()

        for part in range(3):
            left(part)
        part = pl.ds(0, 15 * ROWTILES)
        pltpu.make_async_copy(energy_out.at[part], energy_out.at[part], back_send).wait()
        pltpu.make_async_copy(got.at[part], got.at[part], back_recv).wait()

        for t in range(TILES):
            out_ref[0, :, t * LANES : (t + 1) * LANES] = got[pl.ds(t, 16, stride=ROWTILES), :]


def local(spectral, legendre, wave_map, row_points, brackets, lev_weight, climatology):
    vmem = pl.BlockSpec(memory_space=pltpu.VMEM)
    small = jnp.concatenate([wave_map, row_points, brackets, (lev_weight * SCALE).astype(jnp.int32)])
    hbm = pl.BlockSpec(memory_space=pltpu.HBM)
    rows = SLOTS * PER_SLOT
    f32, bf16, dma = jnp.float32, jnp.bfloat16, pltpu.SemaphoreType.DMA
    energy = pl.pallas_call(
        kernel,
        grid=(STEPS,),
        out_shape=jax.ShapeDtypeStruct((1, 16, ROWPAD), f32),
        in_specs=[
            hbm,
            hbm,
            hbm,
        ],
        out_specs=vmem,
        scratch_shapes=[
            pltpu.SMEM((SMALL,), jnp.int32),
            pltpu.VMEM((SMALL,), jnp.int32),
            dma((2,)),
            pltpu.VMEM((BUFFERS, STEP_SLOTS, LEV_DEV * COLS, NT), bf16),
            pltpu.VMEM((BUFFERS, STEP_SLOTS, HALF, NT), bf16),
            dma((2, BUFFERS)),
            pltpu.VMEM((rows, HALF), f32),
            pltpu.VMEM((rows, HALF), f32),
            pltpu.VMEM((rows, HALF), f32),
            pltpu.VMEM((HALF * PACK, LANES), f32),
            pltpu.VMEM((DEVICES * PACK, LANES), f32),
            pltpu.VMEM((2, M, LANES), f32),
            pltpu.VMEM((M, LANES), bf16),
            pltpu.VMEM((M, 2 * LANES), bf16),
            pltpu.VMEM((M, 2 * LANES), bf16),
            pltpu.VMEM((M, 2 * LANES), bf16),
            pltpu.VMEM((M, 2 * LANES), bf16),
            pltpu.VMEM((KBLOCK, M), f32),
            pltpu.VMEM((KBLOCK, M), f32),
            pltpu.VMEM((16, M), f32),
            pltpu.VMEM((16, M), f32),
            pltpu.VMEM((KSPAN, M), bf16),
            pltpu.VMEM((KSPAN, M), bf16),
            pltpu.VMEM((KSPAN, M), bf16),
            pltpu.VMEM((KSPAN, M), bf16),
            pltpu.VMEM((KSPAN, 4 * LANES), f32),
            pltpu.VMEM((KSPAN, 4 * LANES), bf16),
            pltpu.VMEM((KSPAN, 4 * LANES), bf16),
            pltpu.VMEM((4, KBLOCKS, 16, LANES), f32),
            pltpu.VMEM((16 * ROWTILES, LANES), f32),
            pltpu.VMEM((16 * ROWTILES, LANES), f32),
            dma((STEPS,)),
            dma((STEPS,)),
            dma((3,)),
            dma((3,)),
            dma((3,)),
            dma,
            dma,
            pltpu.SemaphoreType.REGULAR,
        ],
        compiler_params=pltpu.CompilerParams(
            collective_id=0, has_side_effects=True, vmem_limit_bytes=52 * 1024 * 1024
        ),
        name="transform",
    )(small, spectral, legendre)
    return jnp.where(energy < 0.0, 0.0, energy - climatology)


def solution(mesh):
    placed = (
        P("wave", "lev", None),
        P("wave", None, None),
        P(),
        P(),
        P(),
        P(),
        P("lev", "wave", None),
    )
    return jax.shard_map(
        local, mesh=mesh, in_specs=placed, out_specs=P("lev", "wave", None), check_vma=False
    )
```
